32 devices in a mesh: grp: 2 (over x), sta: 16 (over z, y, core).
Axes of the slice: x: 2, y: 2, z: 4, core: 2. Of those that a mesh axis runs over, the one named last changes fastest.
Arguments:
- spectra: bfloat16 [2, 8, 16, 64, 2048], P(None, 'grp', None, 'sta'), parts along dimension 1, may hold values from -6 to 6
- block_counts: int32 [16], replicated, may hold values from 1 to 4, as said below
- window_masks: int32 [8, 16, 16], P('grp'), parts along dimension 0, may hold values from 0 to 1, as said below
- pair_table: int32 [4, 8, 2], replicated, may hold values from 0 to 15, as said below
Outputs:
- stacks: float32 [8, 32, 16, 2048], P('grp', 'sta'), parts along dimension 0
The draws below stay inside these ranges and needn't reach their ends.
There are 2 independent parts, one for each index of `grp`. The reference program is written for one: setup_inputs(seed, part) draws one part's arguments, and reference() takes and returns one part's arrays. A program takes and returns all parts, laid end to end along the dimension named above; an argument that names none is the same for every part. Nothing has to cross between parts.
Inputs may be any that keep to these rules, and one draw needn't show every extreme that they name: `block_counts`: the largest is 4. `window_masks`: some block-days have no valid window. `pair_table`: in each round every block appears in exactly one pair.
All inputs are finite; a program needn't handle non-finite values.
Results may differ from the reference program's by a relative error of at most 0.0038.
Values may be sent and summed in bfloat16 or wider, within the bound.
No kernel may reach another device: no remote copies, remote signals or barrier semaphores. Data moves between devices by JAX's collectives and lax.ppermute only.
A program may use at most 320 MiB of HBM per device.

```python
import math
import jax
import jax.numpy as jnp

F = 2048
LAGS = 2048
S = 4
DAYS = 4
WIN = 16
ROUNDS = 4
NPAIR = 8
STATIONS = 64
N_STA = 16


def draw_block_counts(key, part):
    first_key, second_key = jax.random.split(jax.random.fold_in(key, 11))
    counts = jax.random.randint(first_key, (N_STA,), 1, S + 1)
    fullest = jax.random.randint(second_key, (), 0, N_STA)
    return jnp.where(jnp.arange(N_STA) == fullest, S, counts).astype(jnp.int32)


def draw_window_masks(key, part):
    first_key, second_key = jax.random.split(jax.random.fold_in(key, 23))
    valid = (jax.random.randint(first_key, (DAYS, WIN, N_STA), 0, 4) < 3).astype(jnp.int32)
    rolls = jax.random.randint(second_key, (DAYS, 1, N_STA), 0, 8)
    dead = (rolls == 0) | (jnp.arange(DAYS)[:, None, None] == 0) & (jnp.arange(N_STA)[None, None, :] == 0)
    return jnp.where(dead, 0, valid).astype(jnp.int32)


def draw_pair_table(key, part):
    round_keys = jax.random.split(jax.random.fold_in(key, 37), ROUNDS)
    orders = jax.vmap(lambda round_key: jax.random.permutation(round_key, N_STA))(round_keys)
    return orders.reshape(ROUNDS, N_STA // 2, 2).astype(jnp.int32)


def level_of(key, extent, cuts, low, top_value):
    def one(axis_at, shards_of):
        draws = jax.random.uniform(jax.random.fold_in(jax.random.fold_in(key, 6), axis_at), (shards_of,), jnp.float32, low / len(cuts), top_value / len(cuts))
        return jnp.repeat(jnp.exp(draws), extent[axis_at] // shards_of).reshape((-1,) + (1,) * (len(extent) - axis_at - 1))

    gain = one(*cuts[0])
    for cut in cuts[1:]:
        gain = gain * one(*cut)
    return gain


def centred(key, shape, spread, limit, cuts=(), kind=jnp.bfloat16):
    values = jax.random.normal(key, shape, jnp.float32) * spread
    if len(cuts) > 0:
        values = level_of(key, shape, cuts, -0.22, 0.18) * values
    return jnp.clip(values, min=-limit, max=limit).astype(kind)


def setup_inputs(seed: int = 0, part: int = 0) -> dict:
    streams_of = jax.random.split(jax.random.key(seed), 5)
    part_splits = jax.random.split(jax.random.fold_in(streams_of[4], part), 5)
    spectra = centred(part_splits[0], (2, DAYS, WIN, STATIONS, F), 1.0, 6.0, ((3, 16),))
    block_counts = draw_block_counts(jax.random.fold_in(streams_of[4], 71), part)
    window_masks = draw_window_masks(jax.random.fold_in(jax.random.fold_in(streams_of[4], part), 71), part)
    pair_table = draw_pair_table(jax.random.fold_in(streams_of[4], 71), part)
    return dict(spectra=spectra, block_counts=block_counts, window_masks=window_masks, pair_table=pair_table)


def phase_table(freq_count, lag_count):
    freqs = jnp.arange(freq_count, dtype=jnp.int32)
    shifts = jnp.mod(jnp.arange(lag_count, dtype=jnp.int32) - lag_count // 2, 2 * freq_count)
    phases = jnp.mod(freqs[:, None] * shifts[None, :], 2 * freq_count)
    angles = phases.astype(jnp.float32) * (math.pi / freq_count)
    return jnp.concatenate([jnp.cos(angles), -jnp.sin(angles)], axis=0).astype(jnp.bfloat16)

def cross_round(blocks, weights, first, second):
    left = jnp.take(blocks, first, axis=3)
    right = jnp.take(blocks, second, axis=3)
    pattern = 'dwpif,dwpjf->dpijf'
    real_part = jnp.einsum(pattern, left[0], right[0]) + jnp.einsum(pattern, left[1], right[1])
    imag_part = jnp.einsum(pattern, left[1], right[0]) - jnp.einsum(pattern, left[0], right[1])
    joint = jnp.einsum('dwp,dwp->dp', jnp.take(weights, first, axis=2), jnp.take(weights, second, axis=2))
    inverse = 1.0 / jnp.maximum(joint, 1.0)
    real_part = jnp.cumsum(real_part * inverse[:, :, None, None, None], axis=0)
    imag_part = jnp.cumsum(imag_part * inverse[:, :, None, None, None], axis=0)
    stacked = jnp.stack([real_part, imag_part]).astype(jnp.bfloat16)
    ordered = jnp.transpose(stacked, (2, 1, 3, 4, 0, 5))
    return ordered

def reference(spectra, block_counts, window_masks, pair_table):
    station_ids = jnp.arange(S * N_STA, dtype=jnp.int32)
    owners = station_ids // S
    live_slots = station_ids % S < jnp.take(block_counts, owners)
    keeper = (jnp.take(window_masks, owners, axis=2) > 0) & live_slots[None, None, :]
    cleaned = spectra.astype(jnp.float32) * keeper[None, :, :, :, None].astype(jnp.float32)
    blocks = cleaned.reshape(2, DAYS, WIN, N_STA, S, F)
    weights = window_masks.astype(jnp.float32)
    phase_rows = phase_table(F, LAGS)
    lag_scale = 1.0 / math.sqrt(F)
    results = []
    for round_index in range(ROUNDS):
        ordered = cross_round(blocks, weights, pair_table[round_index, :, 0], pair_table[round_index, :, 1])
        rows = ordered.reshape(-1, 2 * F)
        lagged = jnp.dot(rows, phase_rows, preferred_element_type=jnp.float32) * lag_scale
        results.append(lagged.reshape(NPAIR * DAYS, S * S, LAGS))
    return jnp.stack(results)
```

```python
import functools
import math

import jax
import jax.numpy as jnp
import ml_dtypes
import numpy as np
from jax import lax
from jax.experimental import pallas as pl
from jax.experimental.pallas import tpu as pltpu
from jax.sharding import PartitionSpec as P

LAGS = 2048
MIB = 1 << 20


def phase_table(freq_count, lag_count, devices):
    freqs = np.arange(freq_count, dtype=np.int64)
    shifts = np.mod(np.arange(lag_count, dtype=np.int64) - lag_count // 2, 2 * freq_count)
    phases = np.mod(freqs[:, None] * shifts[None, :], 2 * freq_count)
    angles = np.arange(2 * freq_count) * (math.pi / freq_count)
    cosines = np.cos(angles).astype(np.float32).astype(ml_dtypes.bfloat16)[phases]
    sines = (-np.sin(angles)).astype(np.float32).astype(ml_dtypes.bfloat16)[phases]
    bins = freq_count // devices
    both = np.stack([cosines, sines]).reshape(2, devices, bins, lag_count)
    return np.ascontiguousarray(both.transpose(1, 0, 2, 3)).reshape(2 * freq_count, lag_count)


def pack_kernel(devices, counts_ref, masks_ref, spectra_ref, out_ref, rows_ref):
    me = lax.axis_index("sta")
    windows, slots = spectra_ref.shape[2], spectra_ref.shape[3]
    bins = out_ref.shape[-1]
    count = counts_ref[me]
    lane = lax.broadcasted_iota(jnp.int32, masks_ref.shape[1:], 1)
    mine = jnp.where(lane == me, masks_ref[0], 0)
    keep = (jnp.sum(mine, axis=1, keepdims=True) > 0).astype(jnp.float32)
    for owner in range(devices):
        for w in range(windows):
            rows_ref[owner, w * slots : (w + 1) * slots, :] = spectra_ref[
                0, 0, w, :, owner * bins : (owner + 1) * bins
            ].astype(jnp.float32)
    for slot in range(slots):
        live = keep * jnp.where(slot < count, 1.0, 0.0)
        wide = jnp.broadcast_to(live, (windows, bins))
        for owner in range(devices):
            picked = rows_ref[owner, pl.ds(slot, windows, stride=slots), :]
            out_ref[owner, 0, 0, slot] = (picked * wide).astype(jnp.bfloat16)


def pack(spectra, block_counts, window_masks, devices):
    parts, days, windows, slots, total = spectra.shape
    bins = total // devices
    return pl.pallas_call(
        functools.partial(pack_kernel, devices),
        grid=(parts, days),
        in_specs=[
            pl.BlockSpec(memory_space=pltpu.SMEM),
            pl.BlockSpec((1,) + window_masks.shape[1:], lambda c, d: (d, 0, 0)),
            pl.BlockSpec((1, 1, windows, slots, total), lambda c, d: (c, d, 0, 0, 0)),
        ],
        out_specs=pl.BlockSpec(
            (devices, 1, 1, slots, windows, bins), lambda c, d: (0, c, d, 0, 0, 0)
        ),
        out_shape=jax.ShapeDtypeStruct(
            (devices, parts, days, slots, windows, bins), jnp.bfloat16
        ),
        scratch_shapes=[pltpu.VMEM((devices, windows * slots, bins), jnp.float32)],
        compiler_params=pltpu.CompilerParams(vmem_limit_bytes=32 * MIB),
        name="pack",
    )(block_counts, window_masks, spectra)


def window_sums(terms, rows):
    for step in (1, 2, 4):
        own = (rows & step) == 0
        terms = [
            jnp.where(own, first, second) + pltpu.roll(jnp.where(own, second, first), 8 - step, 0)
            for first, second in zip(terms[::2], terms[1::2])
        ]
    return terms[0]


def cross_kernel(pairs_ref, inverse_ref, blocks_ref, out_ref):
    days, slots = blocks_ref.shape[2], blocks_ref.shape[3]
    bins = blocks_ref.shape[-1]
    block_count = blocks_ref.shape[0]
    rounds, pairs = pairs_ref.shape[0], pairs_ref.shape[1]
    rows = lax.broadcasted_iota(jnp.int32, (8, bins), 0)
    held = days * pairs // block_count

    def one_pair(index, carry):
        r, p = index // pairs, index % pairs
        a, b = pairs_ref[r, p, 0], pairs_ref[r, p, 1]
        total = None
        for d in range(days):
            scale = inverse_ref[(d * block_count + a) * block_count + b]
            left = [[blocks_ref[a, c, d, s].astype(jnp.float32) for s in range(slots)] for c in range(2)]
            right = [[blocks_ref[b, c, d, s].astype(jnp.float32) for s in range(slots)] for c in range(2)]
            fresh = []
            for half in range(slots * slots // 8):
                real, imag = [], []
                for k in range(8):
                    i, j = divmod(half * 8 + k, slots)
                    re = left[0][i] * right[0][j] + left[1][i] * right[1][j]
                    im = left[1][i] * right[0][j] - left[0][i] * right[1][j]
                    real.append(re[:8] + re[8:])
                    imag.append(im[:8] + im[8:])
                fresh.append((window_sums(real, rows) * scale, window_sums(imag, rows) * scale))
            if total is None:
                total = fresh
            else:
                total = [(t[0] + n[0], t[1] + n[1]) for t, n in zip(total, fresh)]
            row = pl.multiple_of(r * held * slots * slots + (d % held) * slots * slots, 16)
            place = (p * days + d) // held
            for c in range(2):
                out_ref[place, c, pl.ds(row, slots * slots), :] = jnp.concatenate(
                    [t[c] for t in total], axis=0
                ).astype(jnp.bfloat16)
        return carry

    lax.fori_loop(0, rounds * pairs, one_pair, 0)


def cross(blocks, inverse, pair_table):
    devices, parts, days, slots, windows, bins = blocks.shape
    rounds, pairs, _ = pair_table.shape
    held = days * pairs // devices
    return pl.pallas_call(
        cross_kernel,
        in_specs=[
            pl.BlockSpec(memory_space=pltpu.SMEM),
            pl.BlockSpec(memory_space=pltpu.SMEM),
            pl.BlockSpec(memory_space=pltpu.VMEM),
        ],
        out_specs=pl.BlockSpec(memory_space=pltpu.VMEM),
        out_shape=jax.ShapeDtypeStruct(
            (devices, parts, rounds * held * slots * slots, bins), jnp.bfloat16
        ),
        compiler_params=pltpu.CompilerParams(vmem_limit_bytes=40 * MIB),
        name="cross",
    )(pair_table, inverse, blocks)


def lag_kernel(scale, stacked_ref, table_ref, out_ref, left_ref):
    devices, parts, rows, bins = stacked_ref.shape

    @pl.when(pl.program_id(0) == 0)
    def _():
        for src in range(devices):
            for c in range(parts):
                at = (src * parts + c) * bins
                left_ref[:, at : at + bins] = stacked_ref[src, c]

    out_ref[...] = (
        jnp.dot(left_ref[...], table_ref[...], preferred_element_type=jnp.float32) * scale
    )


def lags(stacked, table, scale):
    devices, parts, rows, bins = stacked.shape
    depth, lag_count = table.shape
    tile = 256
    return pl.pallas_call(
        functools.partial(lag_kernel, scale),
        grid=(lag_count // tile,),
        in_specs=[
            pl.BlockSpec((devices, parts, rows, bins), lambda t: (0, 0, 0, 0)),
            pl.BlockSpec((depth, tile), lambda t: (0, t)),
        ],
        out_specs=pl.BlockSpec((rows, tile), lambda t: (0, t)),
        out_shape=jax.ShapeDtypeStruct((rows, lag_count), jnp.float32),
        scratch_shapes=[pltpu.VMEM((rows, depth), jnp.bfloat16)],
        compiler_params=pltpu.CompilerParams(vmem_limit_bytes=32 * MIB),
        name="lags",
    )(stacked, table)


def local(table, spectra, block_counts, window_masks, pair_table):
    devices = lax.axis_size("sta")
    parts, days, windows, slots, total = spectra.shape
    rounds, pairs, _ = pair_table.shape
    held = days * pairs // devices
    packed = pack(spectra, block_counts, window_masks, devices)
    blocks = lax.all_to_all(packed, "sta", split_axis=0, concat_axis=0, tiled=True)
    weights = window_masks.astype(jnp.float32)
    joint = jnp.einsum("dwa,dwb->dab", weights, weights)
    inverse = (1.0 / jnp.maximum(joint, 1.0)).reshape(-1)
    stacked = cross(blocks, inverse, pair_table)
    received = lax.all_to_all(stacked, "sta", split_axis=0, concat_axis=0, tiled=True)
    lagged = lags(received, table, 1.0 / math.sqrt(total))
    return lagged.reshape(rounds, held, slots * slots, LAGS)


def solution(mesh):
    devices = mesh.shape["sta"]
    placed = (P(None, "grp", None, "sta", None), P(), P("grp", None, None), P())

    def run(spectra, block_counts, window_masks, pair_table):
        table = phase_table(spectra.shape[-1], LAGS, devices)
        return jax.shard_map(
            functools.partial(local, table),
            mesh=mesh,
            in_specs=placed,
            out_specs=P("grp", "sta", None, None),
            check_vma=False,
        )(spectra, block_counts, window_masks, pair_table)

    return run
```

```python
import functools
import math

import jax
import jax.numpy as jnp
import ml_dtypes
import numpy as np
from jax import lax
from jax.experimental import pallas as pl
from jax.experimental.pallas import tpu as pltpu
from jax.sharding import PartitionSpec as P

LAGS = 2048
MIB = 1 << 20


def phase_tiles(freq_count, lag_count, tile):
    freqs = np.arange(freq_count, dtype=np.int64)
    shifts = np.arange(lag_count // 2, dtype=np.int64)
    phases = np.mod(freqs[:, None] * shifts[None, :], 2 * freq_count)
    angles = np.arange(2 * freq_count) * (math.pi / freq_count)
    cosines = np.cos(angles).astype(np.float32).astype(ml_dtypes.bfloat16)[phases]
    sines = (-np.sin(angles)).astype(np.float32).astype(ml_dtypes.bfloat16)[phases]
    both = np.stack([cosines, sines]).reshape(2, freq_count, -1, tile)
    return np.ascontiguousarray(both.transpose(2, 0, 1, 3))


def pack_kernel(
    devices, counts_ref, masks_ref, spectra_ref, out_ref, raw_ref, rows_ref, ready_ref, in_sems, out_sems
):
    me = lax.axis_index("sta")
    parts, days, windows, slots, _ = spectra_ref.shape
    bins = out_ref.shape[-1]
    count = counts_ref[me]

    def load(step):
        c, d = step // days, step % days
        return pltpu.make_async_copy(spectra_ref.at[c, d], raw_ref.at[c, d], in_sems.at[step])

    def store(step):
        c, d = step // days, step % days
        return pltpu.make_async_copy(ready_ref.at[:, c, d], out_ref.at[:, c, d], out_sems.at[step])

    for step in range(parts * days):
        load(step).start()
    lane = lax.broadcasted_iota(jnp.int32, masks_ref.shape[1:], 1)

    def one(step, carry):
        c, d = step // days, step % days
        mine = jnp.where(lane == me, masks_ref[d], 0)
        keep = (jnp.sum(mine, axis=1, keepdims=True) > 0).astype(jnp.float32)
        load(step).wait()
        for owner in range(devices):
            for w in range(windows):
                rows_ref[owner, w * slots : (w + 1) * slots, :] = raw_ref[
                    c, d, w, :, owner * bins : (owner + 1) * bins
                ].astype(jnp.float32)
        for slot in range(slots):
            live = keep * jnp.where(slot < count, 1.0, 0.0)
            wide = jnp.broadcast_to(live, (windows, bins))
            for owner in range(devices):
                picked = rows_ref[owner, pl.ds(slot, windows, stride=slots), :]
                ready_ref[owner, c, d, slot] = (picked * wide).astype(jnp.bfloat16)
        store(step).start()
        return carry

    lax.fori_loop(0, parts * days, one, 0)
    for step in range(parts * days):
        store(step).wait()


def pack(spectra, block_counts, window_masks, devices):
    parts, days, windows, slots, total = spectra.shape
    bins = total // devices
    packed = (devices, parts, days, slots, windows, bins)
    return pl.pallas_call(
        functools.partial(pack_kernel, devices),
        in_specs=[
            pl.BlockSpec(memory_space=pltpu.SMEM),
            pl.BlockSpec(memory_space=pltpu.VMEM),
            pl.BlockSpec(memory_space=pl.ANY),
        ],
        out_specs=pl.BlockSpec(memory_space=pl.ANY),
        out_shape=jax.ShapeDtypeStruct(packed, jnp.bfloat16),
        scratch_shapes=[
            pltpu.VMEM(spectra.shape, jnp.bfloat16),
            pltpu.VMEM((devices, windows * slots, bins), jnp.float32),
            pltpu.VMEM(packed, jnp.bfloat16),
            pltpu.SemaphoreType.DMA((parts * days,)),
            pltpu.SemaphoreType.DMA((parts * days,)),
        ],
        compiler_params=pltpu.CompilerParams(vmem_limit_bytes=60 * MIB),
        name="pack",
    )(block_counts, window_masks, spectra)


def window_sums(terms, rows):
    for step in (1, 2, 4):
        own = (rows & step) == 0
        terms = [
            jnp.where(own, first, second) + pltpu.roll(jnp.where(own, second, first), 8 - step, 0)
            for first, second in zip(terms[::2], terms[1::2])
        ]
    return terms[0]


def pair_stack(a, b, inverse_ref, blocks_ref, rows):
    block_count, _, days, slots = blocks_ref.shape[:4]
    total = None
    stacked = []
    for d in range(days):
        scale = inverse_ref[(d * block_count + a) * block_count + b]
        right = [[blocks_ref[b, c, d, s].astype(jnp.float32) for s in range(slots)] for c in range(2)]
        right_sum = [x + y for x, y in zip(right[0], right[1])]
        right_gap = [y - x for x, y in zip(right[0], right[1])]
        real, imag = [], []
        for i in range(slots):
            left_real = blocks_ref[a, 0, d, i].astype(jnp.float32)
            left_imag = blocks_ref[a, 1, d, i].astype(jnp.float32)
            left_sum = left_real + left_imag
            for j in range(slots):
                shared = left_sum * right[0][j]
                gain = left_imag * right_gap[j]
                loss = left_real * right_sum[j]
                both = shared[:8] + shared[8:]
                real.append(both + (gain[:8] + gain[8:]))
                imag.append(both - (loss[:8] + loss[8:]))
        fresh = [
            [window_sums(part[k : k + 8], rows) * scale for k in range(0, slots * slots, 8)]
            for part in (real, imag)
        ]
        if total is None:
            total = fresh
        else:
            total = [[t + n for t, n in zip(ts, ns)] for ts, ns in zip(total, fresh)]
        stacked.append([jnp.concatenate(part, axis=0).astype(jnp.bfloat16) for part in total])
    return stacked


def cross_kernel(pairs_ref, inverse_ref, blocks_ref, out_ref):
    block_count, _, days, slots, _, bins = blocks_ref.shape
    rounds, pairs = pairs_ref.shape[0], pairs_ref.shape[1]
    rows = lax.broadcasted_iota(jnp.int32, (8, bins), 0)
    held = days * pairs // block_count

    def one_pair(index, carry):
        r, p = index // pairs, index % pairs
        stacked = pair_stack(pairs_ref[r, p, 0], pairs_ref[r, p, 1], inverse_ref, blocks_ref, rows)
        for d in range(days):
            row = pl.multiple_of((r * held + d % held) * slots * slots, 16)
            for c in range(2):
                out_ref[(p * days + d) // held, c, pl.ds(row, slots * slots), :] = stacked[d][c]
        return carry

    lax.fori_loop(0, rounds * pairs, one_pair, 0)


def cross(blocks, inverse, pair_table):
    devices, parts, days, slots, windows, bins = blocks.shape
    rounds, pairs, _ = pair_table.shape
    held = days * pairs // devices
    return pl.pallas_call(
        cross_kernel,
        in_specs=[
            pl.BlockSpec(memory_space=pltpu.SMEM),
            pl.BlockSpec(memory_space=pltpu.SMEM),
            pl.BlockSpec(memory_space=pltpu.VMEM),
        ],
        out_specs=pl.BlockSpec(memory_space=pltpu.VMEM),
        out_shape=jax.ShapeDtypeStruct(
            (devices, parts, rounds * held * slots * slots, bins), jnp.bfloat16
        ),
        compiler_params=pltpu.CompilerParams(vmem_limit_bytes=16 * MIB),
        name="cross",
    )(pair_table, inverse, blocks)


def lag_kernel(
    scale, stacked_ref, table_ref, out_ref, left_ref, held_ref, lagged_ref, in_sems, out_sems
):
    tiles, _, depth, tile = table_ref.shape
    parts, rows, _ = left_ref.shape
    half = tiles * tile
    loads = [
        pltpu.make_async_copy(table_ref.at[t], held_ref.at[t], in_sems.at[t]) for t in range(tiles)
    ]
    for t in reversed(range(tiles)):
        loads[t].start()
    devices, _, _, bins = stacked_ref.shape
    for c in range(parts):
        for src in range(devices):
            left_ref[c, :, src * bins : (src + 1) * bins] = stacked_ref[src, c]

    turn = lax.broadcasted_iota(jnp.int32, (depth, 128), 0) % 4
    cosine = jnp.where(turn == 0, 1.0, jnp.where(turn == 2, -1.0, 0.0)).astype(jnp.bfloat16)
    sine = jnp.where(turn == 1, 1.0, jnp.where(turn == 3, -1.0, 0.0)).astype(jnp.bfloat16)
    before = jnp.dot(left_ref[0], cosine, preferred_element_type=jnp.float32)
    before = (before + jnp.dot(left_ref[1], sine, preferred_element_type=jnp.float32)) * scale

    lane = lax.broadcasted_iota(jnp.int32, (rows, 128), 1)
    flip = (128 - lane) % 128
    stores = []
    for t in reversed(range(tiles)):
        loads[t].wait()
        even = jnp.dot(left_ref[0], held_ref[t, 0], preferred_element_type=jnp.float32) * scale
        odd = jnp.dot(left_ref[1], held_ref[t, 1], preferred_element_type=jnp.float32) * scale
        lagged_ref[:, half + t * tile : half + (t + 1) * tile] = even + odd
        gap = even - odd
        for sub in reversed(range(tile // 128)):
            turned = jnp.take_along_axis(gap[:, sub * 128 : (sub + 1) * 128], flip, axis=1)
            at = half - t * tile - (sub + 1) * 128
            lagged_ref[:, at : at + 128] = jnp.where(lane == 0, before, turned)
            before = turned
        for k, at in enumerate((half + t * tile, half - (t + 1) * tile)):
            stores.append(
                pltpu.make_async_copy(
                    lagged_ref.at[:, at : at + tile],
                    out_ref.at[:, at : at + tile],
                    out_sems.at[2 * t + k],
                )
            )
            stores[-1].start()
    for store in stores:
        store.wait()


def lags(stacked, table, scale):
    devices, parts, rows, bins = stacked.shape
    tiles, _, depth, tile = table.shape
    lag_count = 2 * tiles * tile
    return pl.pallas_call(
        functools.partial(lag_kernel, scale),
        in_specs=[
            pl.BlockSpec(memory_space=pltpu.VMEM),
            pl.BlockSpec(memory_space=pl.ANY),
        ],
        out_specs=pl.BlockSpec(memory_space=pl.ANY),
        out_shape=jax.ShapeDtypeStruct((rows, lag_count), jnp.float32),
        scratch_shapes=[
            pltpu.VMEM((parts, rows, depth), jnp.bfloat16),
            pltpu.VMEM(table.shape, jnp.bfloat16),
            pltpu.VMEM((rows, lag_count), jnp.float32),
            pltpu.SemaphoreType.DMA((tiles,)),
            pltpu.SemaphoreType.DMA((2 * tiles,)),
        ],
        compiler_params=pltpu.CompilerParams(vmem_limit_bytes=48 * MIB),
        name="lags",
    )(stacked, table)


def local(table, spectra, block_counts, window_masks, pair_table):
    devices = lax.axis_size("sta")
    parts, days, windows, slots, total = spectra.shape
    rounds, pairs, _ = pair_table.shape
    held = days * pairs // devices
    packed = pack(spectra, block_counts, window_masks, devices)
    blocks = lax.all_to_all(packed, "sta", split_axis=0, concat_axis=0, tiled=True)
    weights = window_masks.astype(jnp.float32)
    joint = jnp.einsum("dwa,dwb->dab", weights, weights)
    inverse = (1.0 / jnp.maximum(joint, 1.0)).reshape(-1)
    stacked = cross(blocks, inverse, pair_table)
    received = lax.all_to_all(stacked, "sta", split_axis=0, concat_axis=0, tiled=True)
    lagged = lags(received, table, 1.0 / math.sqrt(total))
    return lagged.reshape(rounds, held, slots * slots, LAGS)


def solution(mesh):
    placed = (P(None, "grp", None, "sta", None), P(), P("grp", None, None), P())

    def run(spectra, block_counts, window_masks, pair_table):
        table = phase_tiles(spectra.shape[-1], LAGS, 256)
        return jax.shard_map(
            functools.partial(local, table),
            mesh=mesh,
            in_specs=placed,
            out_specs=P("grp", "sta", None, None),
            check_vma=False,
        )(spectra, block_counts, window_masks, pair_table)

    return run
```

```python
import functools
import math

import jax
import jax.numpy as jnp
import ml_dtypes
import numpy as np
from jax import lax
from jax.experimental import pallas as pl
from jax.experimental.pallas import tpu as pltpu
from jax.sharding import PartitionSpec as P

LAGS = 2048
MIB = 1 << 20
ORDER = (12, 1, 13, 2, 14, 3, 15, 4, 8, 5, 9, 6, 10, 7, 11)
FIRST = 5


def phase_tiles(freq_count, lag_count, tile):
    freqs = np.arange(freq_count, dtype=np.int64)
    shifts = np.arange(lag_count // 2, dtype=np.int64)
    phases = np.mod(freqs[:, None] * shifts[None, :], 2 * freq_count)
    angles = np.arange(2 * freq_count) * (math.pi / freq_count)
    cosines = np.cos(angles).astype(np.float32).astype(ml_dtypes.bfloat16)[phases]
    sines = (-np.sin(angles)).astype(np.float32).astype(ml_dtypes.bfloat16)[phases]
    both = np.stack([cosines, sines]).reshape(2, freq_count, -1, tile)
    return np.ascontiguousarray(both.transpose(2, 0, 1, 3))


def pack_kernel(
    devices, counts_ref, masks_ref, spectra_ref, out_ref, raw_ref, rows_ref, ready_ref, in_sems, out_sems
):
    me = lax.axis_index("sta")
    parts, days, windows, slots, _ = spectra_ref.shape
    bins = out_ref.shape[-1]
    count = counts_ref[me]

    def load(step):
        c, d = step // days, step % days
        return pltpu.make_async_copy(spectra_ref.at[c, d], raw_ref.at[c, d], in_sems.at[step])

    def store(step):
        c, d = step // days, step % days
        return pltpu.make_async_copy(ready_ref.at[:, c, d], out_ref.at[:, c, d], out_sems.at[step])

    for step in range(parts * days):
        load(step).start()
    lane = lax.broadcasted_iota(jnp.int32, masks_ref.shape[1:], 1)

    def one(step, carry):
        c, d = step // days, step % days
        mine = jnp.where(lane == me, masks_ref[d], 0)
        keep = (jnp.sum(mine, axis=1, keepdims=True) > 0).astype(jnp.float32)
        load(step).wait()
        for owner in range(devices):
            for w in range(windows):
                rows_ref[owner, w * slots : (w + 1) * slots, :] = raw_ref[
                    c, d, w, :, owner * bins : (owner + 1) * bins
                ].astype(jnp.float32)
        for slot in range(slots):
            live = keep * jnp.where(slot < count, 1.0, 0.0)
            wide = jnp.broadcast_to(live, (windows, bins))
            for owner in range(devices):
                picked = rows_ref[owner, pl.ds(slot, windows, stride=slots), :]
                ready_ref[owner, c, d, slot] = (picked * wide).astype(jnp.bfloat16)
        store(step).start()
        return carry

    lax.fori_loop(0, parts * days, one, 0)
    for step in range(parts * days):
        store(step).wait()


def piece_kernel(aways, counts_ref, masks_ref, spectra_ref, *refs):
    out_refs, raw_ref, rows_ref, sems = refs[: len(aways)], refs[-3], refs[-2], refs[-1]
    me = lax.axis_index("sta")
    parts, days, windows, slots, bins = raw_ref.shape[1:]
    count = counts_ref[me]
    loads = []
    for n, away in enumerate(aways):
        columns = pl.ds(pl.multiple_of((me ^ away) * bins, 128), bins)
        loads.append(
            pltpu.make_async_copy(spectra_ref.at[:, :, :, :, columns], raw_ref.at[n], sems.at[n])
        )
        loads[n].start()
    lane = lax.broadcasted_iota(jnp.int32, masks_ref.shape[1:], 1)
    wide = []
    for d in range(days):
        mine = jnp.where(lane == me, masks_ref[d], 0)
        keep = (jnp.sum(mine, axis=1, keepdims=True) > 0).astype(jnp.float32)
        wide.append(jnp.broadcast_to(keep, (windows, bins)))
    live = [jnp.where(slot < count, 1.0, 0.0) for slot in range(slots)]
    for n, out_ref in enumerate(out_refs):
        loads[n].wait()

        def one(c, carry):
            for d in range(days):
                for w in range(windows):
                    rows_ref[d, w * slots : (w + 1) * slots, :] = raw_ref[n, c, d, w].astype(
                        jnp.float32
                    )
                for slot in range(slots):
                    picked = rows_ref[d, pl.ds(slot, windows, stride=slots), :]
                    out_ref[c, d, slot] = (picked * (wide[d] * live[slot])).astype(jnp.bfloat16)
            return carry

        lax.fori_loop(0, parts, one, 0)


def pieces(spectra, block_counts, window_masks, devices, aways, name):
    parts, days, windows, slots, total = spectra.shape
    bins = total // devices
    share = jax.ShapeDtypeStruct((parts, days, slots, windows, bins), jnp.bfloat16)
    return pl.pallas_call(
        functools.partial(piece_kernel, aways),
        in_specs=[
            pl.BlockSpec(memory_space=pltpu.SMEM),
            pl.BlockSpec(memory_space=pltpu.VMEM),
            pl.BlockSpec(memory_space=pl.ANY),
        ],
        out_specs=[pl.BlockSpec(memory_space=pltpu.VMEM)] * len(aways),
        out_shape=[share] * len(aways),
        scratch_shapes=[
            pltpu.VMEM((len(aways), parts, days, windows, slots, bins), jnp.bfloat16),
            pltpu.VMEM((days, windows * slots, bins), jnp.float32),
            pltpu.SemaphoreType.DMA((len(aways),)),
        ],
        compiler_params=pltpu.CompilerParams(vmem_limit_bytes=60 * MIB),
        name=name,
    )(block_counts, window_masks, spectra)


def pack(spectra, block_counts, window_masks, devices):
    parts, days, windows, slots, total = spectra.shape
    bins = total // devices
    packed = (devices, parts, days, slots, windows, bins)
    return pl.pallas_call(
        functools.partial(pack_kernel, devices),
        in_specs=[
            pl.BlockSpec(memory_space=pltpu.SMEM),
            pl.BlockSpec(memory_space=pltpu.VMEM),
            pl.BlockSpec(memory_space=pl.ANY),
        ],
        out_specs=pl.BlockSpec(memory_space=pl.ANY),
        out_shape=jax.ShapeDtypeStruct(packed, jnp.bfloat16),
        scratch_shapes=[
            pltpu.VMEM(spectra.shape, jnp.bfloat16),
            pltpu.VMEM((devices, windows * slots, bins), jnp.float32),
            pltpu.VMEM(packed, jnp.bfloat16),
            pltpu.SemaphoreType.DMA((parts * days,)),
            pltpu.SemaphoreType.DMA((parts * days,)),
        ],
        compiler_params=pltpu.CompilerParams(vmem_limit_bytes=60 * MIB),
        name="pack",
    )(block_counts, window_masks, spectra)


def window_sums(terms, rows):
    for step in (1, 2, 4):
        own = (rows & step) == 0
        terms = [
            jnp.where(own, first, second) + pltpu.roll(jnp.where(own, second, first), 8 - step, 0)
            for first, second in zip(terms[::2], terms[1::2])
        ]
    return terms[0]


def pair_stack(a, b, inverse_ref, blocks_ref, rows):
    block_count, _, days, slots = blocks_ref.shape[:4]
    total = None
    stacked = []
    for d in range(days):
        scale = inverse_ref[(d * block_count + a) * block_count + b]
        right = [[blocks_ref[b, c, d, s].astype(jnp.float32) for s in range(slots)] for c in range(2)]
        right_sum = [x + y for x, y in zip(right[0], right[1])]
        right_gap = [y - x for x, y in zip(right[0], right[1])]
        real, imag = [], []
        for i in range(slots):
            left_real = blocks_ref[a, 0, d, i].astype(jnp.float32)
            left_imag = blocks_ref[a, 1, d, i].astype(jnp.float32)
            left_sum = left_real + left_imag
            for j in range(slots):
                shared = left_sum * right[0][j]
                gain = left_imag * right_gap[j]
                loss = left_real * right_sum[j]
                both = shared[:8] + shared[8:]
                real.append(both + (gain[:8] + gain[8:]))
                imag.append(both - (loss[:8] + loss[8:]))
        fresh = [
            [window_sums(part[k : k + 8], rows) * scale for k in range(0, slots * slots, 8)]
            for part in (real, imag)
        ]
        if total is None:
            total = fresh
        else:
            total = [[t + n for t, n in zip(ts, ns)] for ts, ns in zip(total, fresh)]
        stacked.append([jnp.concatenate(part, axis=0).astype(jnp.bfloat16) for part in total])
    return stacked


def cross_kernel(sources, pairs_ref, inverse_ref, *refs):
    block_refs, out_ref, blocks_ref = refs[: len(sources)], refs[-2], refs[-1]
    block_count, _, days, slots, _, bins = blocks_ref.shape
    rounds, pairs = pairs_ref.shape[0], pairs_ref.shape[1]
    rows = lax.broadcasted_iota(jnp.int32, (8, bins), 0)
    held = days * pairs // block_count
    me = lax.axis_index("sta")
    for ref, source in zip(block_refs, sources):
        if source is None:

            def widen(n, carry):
                blocks_ref[n] = ref[n].astype(jnp.float32)
                return carry

            lax.fori_loop(0, block_count, widen, 0)
        else:
            blocks_ref[me ^ source] = ref[...].astype(jnp.float32)

    def one_pair(index, carry):
        r, p = index // pairs, index % pairs
        stacked = pair_stack(pairs_ref[r, p, 0], pairs_ref[r, p, 1], inverse_ref, blocks_ref, rows)
        for d in range(days):
            row = pl.multiple_of((r * held + d % held) * slots * slots, 16)
            for c in range(2):
                out_ref[(p * days + d) // held, c, pl.ds(row, slots * slots), :] = stacked[d][c]
        return carry

    lax.fori_loop(0, rounds * pairs, one_pair, 0, unroll=2)


def cross(blocks, sources, inverse, pair_table, devices):
    parts, days, slots, windows, bins = blocks[0].shape[-5:]
    rounds, pairs, _ = pair_table.shape
    held = days * pairs // devices
    return pl.pallas_call(
        functools.partial(cross_kernel, sources),
        in_specs=[pl.BlockSpec(memory_space=pltpu.SMEM)] * 2
        + [pl.BlockSpec(memory_space=pltpu.VMEM)] * len(blocks),
        out_specs=pl.BlockSpec(memory_space=pltpu.VMEM),
        out_shape=jax.ShapeDtypeStruct(
            (devices, parts, rounds * held * slots * slots, bins), jnp.bfloat16
        ),
        scratch_shapes=[pltpu.VMEM((devices, parts, days, slots, windows, bins), jnp.float32)],
        compiler_params=pltpu.CompilerParams(vmem_limit_bytes=40 * MIB),
        name="cross",
    )(pair_table, inverse, *blocks)


def lag_kernel(
    scale, stacked_ref, table_ref, out_ref, left_ref, held_ref, lagged_ref, in_sems, out_sems
):
    tiles, _, depth, tile = table_ref.shape
    parts, rows, _ = left_ref.shape
    half = tiles * tile
    loads = [
        pltpu.make_async_copy(table_ref.at[t], held_ref.at[t], in_sems.at[t]) for t in range(tiles)
    ]
    for t in reversed(range(tiles)):
        loads[t].start()
    devices, _, _, bins = stacked_ref.shape
    for c in range(parts):
        for src in range(devices):
            left_ref[c, :, src * bins : (src + 1) * bins] = stacked_ref[src, c]

    turn = lax.broadcasted_iota(jnp.int32, (depth, 128), 0) % 4
    cosine = jnp.where(turn == 0, 1.0, jnp.where(turn == 2, -1.0, 0.0)).astype(jnp.bfloat16)
    sine = jnp.where(turn == 1, 1.0, jnp.where(turn == 3, -1.0, 0.0)).astype(jnp.bfloat16)
    before = jnp.dot(left_ref[0], cosine, preferred_element_type=jnp.float32)
    before = (before + jnp.dot(left_ref[1], sine, preferred_element_type=jnp.float32)) * scale

    lane = lax.broadcasted_iota(jnp.int32, (rows, 128), 1)
    flip = (128 - lane) % 128
    stores = []
    for t in reversed(range(tiles)):
        loads[t].wait()
        even = jnp.dot(left_ref[0], held_ref[t, 0], preferred_element_type=jnp.float32) * scale
        odd = jnp.dot(left_ref[1], held_ref[t, 1], preferred_element_type=jnp.float32) * scale
        lagged_ref[:, half + t * tile : half + (t + 1) * tile] = even + odd
        gap = even - odd
        for sub in reversed(range(tile // 128)):
            turned = jnp.take_along_axis(gap[:, sub * 128 : (sub + 1) * 128], flip, axis=1)
            at = half - t * tile - (sub + 1) * 128
            lagged_ref[:, at : at + 128] = jnp.where(lane == 0, before, turned)
            before = turned
        for k, at in enumerate((half + t * tile, half - (t + 1) * tile)):
            stores.append(
                pltpu.make_async_copy(
                    lagged_ref.at[:, at : at + tile],
                    out_ref.at[:, at : at + tile],
                    out_sems.at[2 * t + k],
                )
            )
            stores[-1].start()
    for store in stores:
        store.wait()


def lags(stacked, table, scale):
    devices, parts, rows, bins = stacked.shape
    tiles, _, depth, tile = table.shape
    lag_count = 2 * tiles * tile
    return pl.pallas_call(
        functools.partial(lag_kernel, scale),
        in_specs=[
            pl.BlockSpec(memory_space=pltpu.VMEM),
            pl.BlockSpec(memory_space=pl.ANY),
        ],
        out_specs=pl.BlockSpec(memory_space=pl.ANY),
        out_shape=jax.ShapeDtypeStruct((rows, lag_count), jnp.float32),
        scratch_shapes=[
            pltpu.VMEM((parts, rows, depth), jnp.bfloat16),
            pltpu.VMEM(table.shape, jnp.bfloat16),
            pltpu.VMEM((rows, lag_count), jnp.float32),
            pltpu.SemaphoreType.DMA((tiles,)),
            pltpu.SemaphoreType.DMA((2 * tiles,)),
        ],
        compiler_params=pltpu.CompilerParams(vmem_limit_bytes=48 * MIB),
        name="lags",
    )(stacked, table)


def local(table, spectra, block_counts, window_masks, pair_table):
    devices = lax.axis_size("sta")
    parts, days, windows, slots, total = spectra.shape
    rounds, pairs, _ = pair_table.shape
    held = days * pairs // devices
    if devices == len(ORDER) + 1 and total % (128 * devices) == 0:
        sources = ORDER + (0,)
        shares = pieces(spectra, block_counts, window_masks, devices, sources[:FIRST], "pack_first")
        shares += pieces(spectra, block_counts, window_masks, devices, sources[FIRST:], "pack_rest")
        blocks = [
            lax.ppermute(share, "sta", [(n, n ^ away) for n in range(devices)]) if away else share
            for share, away in zip(shares, sources)
        ]
    else:
        packed = pack(spectra, block_counts, window_masks, devices)
        sources = (None,)
        blocks = [lax.all_to_all(packed, "sta", split_axis=0, concat_axis=0, tiled=True)]
    weights = window_masks.astype(jnp.float32)
    joint = jnp.einsum("dwa,dwb->dab", weights, weights)
    inverse = (1.0 / jnp.maximum(joint, 1.0)).reshape(-1)
    stacked = cross(blocks, sources, inverse, pair_table, devices)
    received = lax.all_to_all(stacked, "sta", split_axis=0, concat_axis=0, tiled=True)
    lagged = lags(received, table, 1.0 / math.sqrt(total))
    return lagged.reshape(rounds, held, slots * slots, LAGS)


def solution(mesh):
    placed = (P(None, "grp", None, "sta", None), P(), P("grp", None, None), P())

    def run(spectra, block_counts, window_masks, pair_table):
        table = phase_tiles(spectra.shape[-1], LAGS, 256)
        return jax.shard_map(
            functools.partial(local, table),
            mesh=mesh,
            in_specs=placed,
            out_specs=P("grp", "sta", None, None),
            check_vma=False,
        )(spectra, block_counts, window_masks, pair_table)

    return run
```

```python
import functools
import math

import jax
import jax.numpy as jnp
import ml_dtypes
import numpy as np
from jax import lax
from jax.experimental import pallas as pl
from jax.experimental.pallas import tpu as pltpu
from jax.sharding import PartitionSpec as P

LAGS = 2048
MIB = 1 << 20
ORDER = (12, 1, 13, 2, 14, 3, 15, 4, 8, 5, 9, 6, 10, 7, 11)
FIRST = 5
LATE = 3


def phase_tiles(freq_count, lag_count, tile):
    freqs = np.arange(freq_count, dtype=np.int64)
    shifts = np.arange(lag_count // 2, dtype=np.int64)
    phases = np.mod(freqs[:, None] * shifts[None, :], 2 * freq_count)
    angles = np.arange(2 * freq_count) * (math.pi / freq_count)
    cosines = np.cos(angles).astype(np.float32).astype(ml_dtypes.bfloat16)[phases]
    sines = (-np.sin(angles)).astype(np.float32).astype(ml_dtypes.bfloat16)[phases]
    both = np.stack([cosines, sines]).reshape(2, freq_count, -1, tile)
    return np.ascontiguousarray(both.transpose(2, 0, 1, 3))


def pack_kernel(
    devices, counts_ref, masks_ref, spectra_ref, out_ref, raw_ref, rows_ref, ready_ref, in_sems, out_sems
):
    me = lax.axis_index("sta")
    parts, days, windows, slots, _ = spectra_ref.shape
    bins = out_ref.shape[-1]
    count = counts_ref[me]

    def load(step):
        c, d = step // days, step % days
        return pltpu.make_async_copy(spectra_ref.at[c, d], raw_ref.at[c, d], in_sems.at[step])

    def store(step):
        c, d = step // days, step % days
        return pltpu.make_async_copy(ready_ref.at[:, c, d], out_ref.at[:, c, d], out_sems.at[step])

    for step in range(parts * days):
        load(step).start()
    lane = lax.broadcasted_iota(jnp.int32, masks_ref.shape[1:], 1)

    def one(step, carry):
        c, d = step // days, step % days
        mine = jnp.where(lane == me, masks_ref[d], 0)
        keep = (jnp.sum(mine, axis=1, keepdims=True) > 0).astype(jnp.float32)
        load(step).wait()
        for owner in range(devices):
            for w in range(windows):
                rows_ref[owner, w * slots : (w + 1) * slots, :] = raw_ref[
                    c, d, w, :, owner * bins : (owner + 1) * bins
                ].astype(jnp.float32)
        for slot in range(slots):
            live = keep * jnp.where(slot < count, 1.0, 0.0)
            wide = jnp.broadcast_to(live, (windows, bins))
            for owner in range(devices):
                picked = rows_ref[owner, pl.ds(slot, windows, stride=slots), :]
                ready_ref[owner, c, d, slot] = (picked * wide).astype(jnp.bfloat16)
        store(step).start()
        return carry

    lax.fori_loop(0, parts * days, one, 0)
    for step in range(parts * days):
        store(step).wait()


def piece_kernel(aways, counts_ref, masks_ref, spectra_ref, *refs):
    out_refs, raw_ref, rows_ref, sems = refs[: len(aways)], refs[-3], refs[-2], refs[-1]
    me = lax.axis_index("sta")
    parts, days, windows, slots, bins = raw_ref.shape[1:]
    count = counts_ref[me]
    loads = []
    for n, away in enumerate(aways):
        columns = pl.ds(pl.multiple_of((me ^ away) * bins, 128), bins)
        loads.append(
            pltpu.make_async_copy(spectra_ref.at[:, :, :, :, columns], raw_ref.at[n], sems.at[n])
        )
        loads[n].start()
    lane = lax.broadcasted_iota(jnp.int32, masks_ref.shape[1:], 1)
    wide = []
    for d in range(days):
        mine = jnp.where(lane == me, masks_ref[d], 0)
        keep = (jnp.sum(mine, axis=1, keepdims=True) > 0).astype(jnp.float32)
        wide.append(jnp.broadcast_to(keep, (windows, bins)))
    live = [jnp.where(slot < count, 1.0, 0.0) for slot in range(slots)]
    for n, out_ref in enumerate(out_refs):
        loads[n].wait()

        def one(c, carry):
            for d in range(days):
                for w in range(windows):
                    rows_ref[d, w * slots : (w + 1) * slots, :] = raw_ref[n, c, d, w].astype(
                        jnp.float32
                    )
                for slot in range(slots):
                    picked = rows_ref[d, pl.ds(slot, windows, stride=slots), :]
                    out_ref[c, d, slot] = (picked * (wide[d] * live[slot])).astype(jnp.bfloat16)
            return carry

        lax.fori_loop(0, parts, one, 0)


def pieces(spectra, block_counts, window_masks, devices, aways, name):
    parts, days, windows, slots, total = spectra.shape
    bins = total // devices
    share = jax.ShapeDtypeStruct((parts, days, slots, windows, bins), jnp.bfloat16)
    return pl.pallas_call(
        functools.partial(piece_kernel, aways),
        in_specs=[
            pl.BlockSpec(memory_space=pltpu.SMEM),
            pl.BlockSpec(memory_space=pltpu.VMEM),
            pl.BlockSpec(memory_space=pl.ANY),
        ],
        out_specs=[pl.BlockSpec(memory_space=pltpu.VMEM)] * len(aways),
        out_shape=[share] * len(aways),
        scratch_shapes=[
            pltpu.VMEM((len(aways), parts, days, windows, slots, bins), jnp.bfloat16),
            pltpu.VMEM((days, windows * slots, bins), jnp.float32),
            pltpu.SemaphoreType.DMA((len(aways),)),
        ],
        compiler_params=pltpu.CompilerParams(vmem_limit_bytes=60 * MIB),
        name=name,
    )(block_counts, window_masks, spectra)


def pack(spectra, block_counts, window_masks, devices):
    parts, days, windows, slots, total = spectra.shape
    bins = total // devices
    packed = (devices, parts, days, slots, windows, bins)
    return pl.pallas_call(
        functools.partial(pack_kernel, devices),
        in_specs=[
            pl.BlockSpec(memory_space=pltpu.SMEM),
            pl.BlockSpec(memory_space=pltpu.VMEM),
            pl.BlockSpec(memory_space=pl.ANY),
        ],
        out_specs=pl.BlockSpec(memory_space=pl.ANY),
        out_shape=jax.ShapeDtypeStruct(packed, jnp.bfloat16),
        scratch_shapes=[
            pltpu.VMEM(spectra.shape, jnp.bfloat16),
            pltpu.VMEM((devices, windows * slots, bins), jnp.float32),
            pltpu.VMEM(packed, jnp.bfloat16),
            pltpu.SemaphoreType.DMA((parts * days,)),
            pltpu.SemaphoreType.DMA((parts * days,)),
        ],
        compiler_params=pltpu.CompilerParams(vmem_limit_bytes=60 * MIB),
        name="pack",
    )(block_counts, window_masks, spectra)


def window_sums(terms, rows):
    for step in (1, 2, 4):
        own = (rows & step) == 0
        terms = [
            jnp.where(own, first, second) + pltpu.roll(jnp.where(own, second, first), 8 - step, 0)
            for first, second in zip(terms[::2], terms[1::2])
        ]
    return terms[0]


def pair_stack(a, b, inverse_ref, blocks_ref, rows):
    block_count, _, days, slots = blocks_ref.shape[:4]
    total = None
    stacked = []
    for d in range(days):
        scale = inverse_ref[(d * block_count + a) * block_count + b]
        right = [[blocks_ref[b, c, d, s].astype(jnp.float32) for s in range(slots)] for c in range(2)]
        right_sum = [x + y for x, y in zip(right[0], right[1])]
        right_gap = [y - x for x, y in zip(right[0], right[1])]
        real, imag = [], []
        for i in range(slots):
            left_real = blocks_ref[a, 0, d, i].astype(jnp.float32)
            left_imag = blocks_ref[a, 1, d, i].astype(jnp.float32)
            left_sum = left_real + left_imag
            for j in range(slots):
                shared = left_sum * right[0][j]
                gain = left_imag * right_gap[j]
                loss = left_real * right_sum[j]
                both = shared[:8] + shared[8:]
                real.append(both + (gain[:8] + gain[8:]))
                imag.append(both - (loss[:8] + loss[8:]))
        fresh = [
            [window_sums(part[k : k + 8], rows) * scale for k in range(0, slots * slots, 8)]
            for part in (real, imag)
        ]
        if total is None:
            total = fresh
        else:
            total = [[t + n for t, n in zip(ts, ns)] for ts, ns in zip(total, fresh)]
        stacked.append([jnp.concatenate(part, axis=0).astype(jnp.bfloat16) for part in total])
    return stacked


def cross_kernel(sources, late, aliased, pairs_ref, inverse_ref, *refs):
    block_refs = refs[: len(sources)]
    out_ref, blocks_ref = refs[len(sources) + aliased :]
    block_count, _, days, slots, _, bins = blocks_ref.shape
    rounds, pairs = pairs_ref.shape[0], pairs_ref.shape[1]
    rows = lax.broadcasted_iota(jnp.int32, (8, bins), 0)
    held = days * pairs // block_count
    me = lax.axis_index("sta")
    for ref, source in zip(block_refs, sources):
        if source is None:

            def widen(n, carry):
                blocks_ref[n] = ref[n].astype(jnp.float32)
                return carry

            lax.fori_loop(0, block_count, widen, 0)
        else:
            blocks_ref[me ^ source] = ref[...].astype(jnp.float32)

    def one_pair(index, carry):
        r, p = index // pairs, index % pairs
        a, b = pairs_ref[r, p, 0], pairs_ref[r, p, 1]

        def work():
            stacked = pair_stack(a, b, inverse_ref, blocks_ref, rows)
            for d in range(days):
                row = pl.multiple_of((r * held + d % held) * slots * slots, 16)
                for c in range(2):
                    out_ref[(p * days + d) // held, c, pl.ds(row, slots * slots), :] = stacked[d][c]

        if len(late) == 0 and aliased == 0:
            work()
        else:
            waits = [(x ^ me) == away for x in (a, b) for away in late or sources]
            waits = functools.reduce(jnp.logical_or, waits)
            pl.when(jnp.logical_not(waits) if late else waits)(work)
        return carry

    lax.fori_loop(0, rounds * pairs, one_pair, 0)


def cross(blocks, sources, inverse, pair_table, devices, late=(), started=()):
    parts, days, slots, windows, bins = blocks[0].shape[-5:]
    rounds, pairs, _ = pair_table.shape
    held = days * pairs // devices
    share = len(sources) / devices
    work = int(rounds * pairs * days * slots * slots * windows * bins * share)
    return pl.pallas_call(
        functools.partial(cross_kernel, sources, late, len(started)),
        in_specs=[pl.BlockSpec(memory_space=pltpu.SMEM)] * 2
        + [pl.BlockSpec(memory_space=pltpu.VMEM)] * (len(blocks) + len(started)),
        out_specs=[pl.BlockSpec(memory_space=pltpu.VMEM)] * 2,
        out_shape=[
            jax.ShapeDtypeStruct(
                (devices, parts, rounds * held * slots * slots, bins), jnp.bfloat16
            ),
            jax.ShapeDtypeStruct((devices, parts, days, slots, windows, bins), jnp.float32),
        ],
        input_output_aliases={2 + len(blocks) + n: n for n in range(len(started))},
        compiler_params=pltpu.CompilerParams(vmem_limit_bytes=40 * MIB),
        cost_estimate=pl.CostEstimate(
            flops=16 * work, bytes_accessed=4 << 20, transcendentals=0
        ),
        name="cross_rest" if started else "cross",
    )(pair_table, inverse, *blocks, *started)


def lag_kernel(
    scale, stacked_ref, table_ref, out_ref, left_ref, held_ref, lagged_ref, in_sems, out_sems
):
    tiles, _, depth, tile = table_ref.shape
    parts, rows, _ = left_ref.shape
    half = tiles * tile
    loads = [
        pltpu.make_async_copy(table_ref.at[t], held_ref.at[t], in_sems.at[t]) for t in range(tiles)
    ]
    for t in reversed(range(tiles)):
        loads[t].start()
    devices, _, _, bins = stacked_ref.shape
    for c in range(parts):
        for src in range(devices):
            left_ref[c, :, src * bins : (src + 1) * bins] = stacked_ref[src, c]

    turn = lax.broadcasted_iota(jnp.int32, (depth, 128), 0) % 4
    cosine = jnp.where(turn == 0, 1.0, jnp.where(turn == 2, -1.0, 0.0)).astype(jnp.bfloat16)
    sine = jnp.where(turn == 1, 1.0, jnp.where(turn == 3, -1.0, 0.0)).astype(jnp.bfloat16)
    before = jnp.dot(left_ref[0], cosine, preferred_element_type=jnp.float32)
    before = (before + jnp.dot(left_ref[1], sine, preferred_element_type=jnp.float32)) * scale

    lane = lax.broadcasted_iota(jnp.int32, (rows, 128), 1)
    flip = (128 - lane) % 128
    stores = []
    for t in reversed(range(tiles)):
        loads[t].wait()
        even = jnp.dot(left_ref[0], held_ref[t, 0], preferred_element_type=jnp.float32) * scale
        odd = jnp.dot(left_ref[1], held_ref[t, 1], preferred_element_type=jnp.float32) * scale
        lagged_ref[:, half + t * tile : half + (t + 1) * tile] = even + odd
        gap = even - odd
        for sub in reversed(range(tile // 128)):
            turned = jnp.take_along_axis(gap[:, sub * 128 : (sub + 1) * 128], flip, axis=1)
            at = half - t * tile - (sub + 1) * 128
            lagged_ref[:, at : at + 128] = jnp.where(lane == 0, before, turned)
            before = turned
        for k, at in enumerate((half + t * tile, half - (t + 1) * tile)):
            stores.append(
                pltpu.make_async_copy(
                    lagged_ref.at[:, at : at + tile],
                    out_ref.at[:, at : at + tile],
                    out_sems.at[2 * t + k],
                )
            )
            stores[-1].start()
    for store in stores:
        store.wait()


def lags(stacked, table, scale):
    devices, parts, rows, bins = stacked.shape
    tiles, _, depth, tile = table.shape
    lag_count = 2 * tiles * tile
    return pl.pallas_call(
        functools.partial(lag_kernel, scale),
        in_specs=[
            pl.BlockSpec(memory_space=pltpu.VMEM),
            pl.BlockSpec(memory_space=pl.ANY),
        ],
        out_specs=pl.BlockSpec(memory_space=pl.ANY),
        out_shape=jax.ShapeDtypeStruct((rows, lag_count), jnp.float32),
        scratch_shapes=[
            pltpu.VMEM((parts, rows, depth), jnp.bfloat16),
            pltpu.VMEM(table.shape, jnp.bfloat16),
            pltpu.VMEM((rows, lag_count), jnp.float32),
            pltpu.SemaphoreType.DMA((tiles,)),
            pltpu.SemaphoreType.DMA((2 * tiles,)),
        ],
        compiler_params=pltpu.CompilerParams(vmem_limit_bytes=48 * MIB),
        name="lags",
    )(stacked, table)


def local(table, spectra, block_counts, window_masks, pair_table):
    devices = lax.axis_size("sta")
    parts, days, windows, slots, total = spectra.shape
    rounds, pairs, _ = pair_table.shape
    held = days * pairs // devices
    if devices == len(ORDER) + 1 and total % (128 * devices) == 0:
        sources = ORDER + (0,)
        shares = pieces(spectra, block_counts, window_masks, devices, sources[:FIRST], "pack_first")
        shares += pieces(spectra, block_counts, window_masks, devices, sources[FIRST:], "pack_rest")
        blocks = []
        for n, (share, away) in enumerate(zip(shares, sources)):
            if 5 <= n < len(ORDER):
                share, _ = lax.optimization_barrier((share, blocks[n - 5]))
            if away:
                share = lax.ppermute(share, "sta", [(m, m ^ away) for m in range(devices)])
            blocks.append(share)
    else:
        packed = pack(spectra, block_counts, window_masks, devices)
        sources = (None,)
        blocks = [lax.all_to_all(packed, "sta", split_axis=0, concat_axis=0, tiled=True)]
    weights = window_masks.astype(jnp.float32)
    joint = jnp.einsum("dwa,dwb->dab", weights, weights)
    inverse = (1.0 / jnp.maximum(joint, 1.0)).reshape(-1)
    if len(sources) > 1:
        late = sources[-1 - LATE : -1]
        soon = [n for n, away in enumerate(sources) if away not in late]
        started = cross(
            [blocks[n] for n in soon],
            tuple(sources[n] for n in soon),
            inverse,
            pair_table,
            devices,
            late,
        )
        stacked, _ = cross(
            blocks[-1 - LATE : -1], late, inverse, pair_table, devices, (), tuple(started)
        )
    else:
        stacked, _ = cross(blocks, sources, inverse, pair_table, devices)
    received = lax.all_to_all(stacked, "sta", split_axis=0, concat_axis=0, tiled=True)
    lagged = lags(received, table, 1.0 / math.sqrt(total))
    return lagged.reshape(rounds, held, slots * slots, LAGS)


def solution(mesh):
    placed = (P(None, "grp", None, "sta", None), P(), P("grp", None, None), P())

    def run(spectra, block_counts, window_masks, pair_table):
        table = phase_tiles(spectra.shape[-1], LAGS, 256)
        return jax.shard_map(
            functools.partial(local, table),
            mesh=mesh,
            in_specs=placed,
            out_specs=P("grp", "sta", None, None),
            check_vma=False,
        )(spectra, block_counts, window_masks, pair_table)

    return run
```

```python
import functools
import math

import jax
import jax.numpy as jnp
import ml_dtypes
import numpy as np
from jax import lax
from jax.experimental import pallas as pl
from jax.experimental.pallas import tpu as pltpu
from jax.sharding import PartitionSpec as P

LAGS = 2048
MIB = 1 << 20
ORDER = (12, 1, 13, 2, 14, 3, 15, 4, 8, 5, 9, 6, 10, 7, 11)
FIRST = 5
LATE = 3


def phase_tiles(freq_count, lag_count, tile):
    freqs = np.arange(freq_count, dtype=np.int64)
    shifts = np.arange(lag_count // 2, dtype=np.int64)
    phases = np.mod(freqs[:, None] * shifts[None, :], 2 * freq_count)
    angles = np.arange(2 * freq_count) * (math.pi / freq_count)
    cosines = np.cos(angles).astype(np.float32).astype(ml_dtypes.bfloat16)[phases]
    sines = (-np.sin(angles)).astype(np.float32).astype(ml_dtypes.bfloat16)[phases]
    both = np.stack([cosines, sines]).reshape(2, freq_count, -1, tile)
    return np.ascontiguousarray(both.transpose(2, 0, 1, 3))


def pack_kernel(
    devices, counts_ref, masks_ref, spectra_ref, out_ref, raw_ref, rows_ref, ready_ref, in_sems, out_sems
):
    me = lax.axis_index("sta")
    parts, days, windows, slots, _ = spectra_ref.shape
    bins = out_ref.shape[-1]
    count = counts_ref[me]

    def load(step):
        c, d = step // days, step % days
        return pltpu.make_async_copy(spectra_ref.at[c, d], raw_ref.at[c, d], in_sems.at[step])

    def store(step):
        c, d = step // days, step % days
        return pltpu.make_async_copy(ready_ref.at[:, c, d], out_ref.at[:, c, d], out_sems.at[step])

    for step in range(parts * days):
        load(step).start()
    lane = lax.broadcasted_iota(jnp.int32, masks_ref.shape[1:], 1)

    def one(step, carry):
        c, d = step // days, step % days
        mine = jnp.where(lane == me, masks_ref[d], 0)
        keep = (jnp.sum(mine, axis=1, keepdims=True) > 0).astype(jnp.float32)
        load(step).wait()
        for owner in range(devices):
            for w in range(windows):
                rows_ref[owner, w * slots : (w + 1) * slots, :] = raw_ref[
                    c, d, w, :, owner * bins : (owner + 1) * bins
                ].astype(jnp.float32)
        for slot in range(slots):
            live = keep * jnp.where(slot < count, 1.0, 0.0)
            wide = jnp.broadcast_to(live, (windows, bins))
            for owner in range(devices):
                picked = rows_ref[owner, pl.ds(slot, windows, stride=slots), :]
                ready_ref[owner, c, d, slot] = (picked * wide).astype(jnp.bfloat16)
        store(step).start()
        return carry

    lax.fori_loop(0, parts * days, one, 0)
    for step in range(parts * days):
        store(step).wait()


def piece_kernel(aways, counts_ref, masks_ref, spectra_ref, *refs):
    out_refs, raw_ref, rows_ref, sems = refs[: len(aways)], refs[-3], refs[-2], refs[-1]
    me = lax.axis_index("sta")
    parts, days, windows, slots, bins = raw_ref.shape[1:]
    count = counts_ref[me]
    loads = []
    for n, away in enumerate(aways):
        columns = pl.ds(pl.multiple_of((me ^ away) * bins, 128), bins)
        loads.append(
            pltpu.make_async_copy(spectra_ref.at[:, :, :, :, columns], raw_ref.at[n], sems.at[n])
        )
        loads[n].start()
    lane = lax.broadcasted_iota(jnp.int32, masks_ref.shape[1:], 1)
    wide = []
    for d in range(days):
        mine = jnp.where(lane == me, masks_ref[d], 0)
        keep = (jnp.sum(mine, axis=1, keepdims=True) > 0).astype(jnp.float32)
        wide.append(jnp.broadcast_to(keep, (windows, bins)))
    live = [jnp.where(slot < count, 1.0, 0.0) for slot in range(slots)]
    for n, out_ref in enumerate(out_refs):
        loads[n].wait()

        def one(c, carry):
            for d in range(days):
                for w in range(windows):
                    rows_ref[d, w * slots : (w + 1) * slots, :] = raw_ref[n, c, d, w].astype(
                        jnp.float32
                    )
                for slot in range(slots):
                    picked = rows_ref[d, pl.ds(slot, windows, stride=slots), :]
                    out_ref[c, d, slot] = (picked * (wide[d] * live[slot])).astype(jnp.bfloat16)
            return carry

        lax.fori_loop(0, parts, one, 0)


def pieces(spectra, block_counts, window_masks, devices, aways, name):
    parts, days, windows, slots, total = spectra.shape
    bins = total // devices
    share = jax.ShapeDtypeStruct((parts, days, slots, windows, bins), jnp.bfloat16)
    return pl.pallas_call(
        functools.partial(piece_kernel, aways),
        in_specs=[
            pl.BlockSpec(memory_space=pltpu.SMEM),
            pl.BlockSpec(memory_space=pltpu.VMEM),
            pl.BlockSpec(memory_space=pl.ANY),
        ],
        out_specs=[pl.BlockSpec(memory_space=pltpu.VMEM)] * len(aways),
        out_shape=[share] * len(aways),
        scratch_shapes=[
            pltpu.VMEM((len(aways), parts, days, windows, slots, bins), jnp.bfloat16),
            pltpu.VMEM((days, windows * slots, bins), jnp.float32),
            pltpu.SemaphoreType.DMA((len(aways),)),
        ],
        compiler_params=pltpu.CompilerParams(vmem_limit_bytes=60 * MIB),
        name=name,
    )(block_counts, window_masks, spectra)


def pack(spectra, block_counts, window_masks, devices):
    parts, days, windows, slots, total = spectra.shape
    bins = total // devices
    packed = (devices, parts, days, slots, windows, bins)
    return pl.pallas_call(
        functools.partial(pack_kernel, devices),
        in_specs=[
            pl.BlockSpec(memory_space=pltpu.SMEM),
            pl.BlockSpec(memory_space=pltpu.VMEM),
            pl.BlockSpec(memory_space=pl.ANY),
        ],
        out_specs=pl.BlockSpec(memory_space=pl.ANY),
        out_shape=jax.ShapeDtypeStruct(packed, jnp.bfloat16),
        scratch_shapes=[
            pltpu.VMEM(spectra.shape, jnp.bfloat16),
            pltpu.VMEM((devices, windows * slots, bins), jnp.float32),
            pltpu.VMEM(packed, jnp.bfloat16),
            pltpu.SemaphoreType.DMA((parts * days,)),
            pltpu.SemaphoreType.DMA((parts * days,)),
        ],
        compiler_params=pltpu.CompilerParams(vmem_limit_bytes=60 * MIB),
        name="pack",
    )(block_counts, window_masks, spectra)


def window_sums(terms, rows):
    for step in (1, 2, 4):
        own = (rows & step) == 0
        terms = [
            jnp.where(own, first, second) + pltpu.roll(jnp.where(own, second, first), 8 - step, 0)
            for first, second in zip(terms[::2], terms[1::2])
        ]
    return terms[0]


def pair_stack(a, b, inverse_ref, blocks_ref, rows):
    block_count, _, days, slots = blocks_ref.shape[:4]
    total = None
    stacked = []
    for d in range(days):
        scale = inverse_ref[(d * block_count + a) * block_count + b]
        right = [[blocks_ref[b, c, d, s].astype(jnp.float32) for s in range(slots)] for c in range(2)]
        right_sum = [x + y for x, y in zip(right[0], right[1])]
        right_gap = [y - x for x, y in zip(right[0], right[1])]
        real, imag = [], []
        for i in range(slots):
            left_real = blocks_ref[a, 0, d, i].astype(jnp.float32)
            left_imag = blocks_ref[a, 1, d, i].astype(jnp.float32)
            left_sum = left_real + left_imag
            for j in range(slots):
                shared = left_sum * right[0][j]
                gain = left_imag * right_gap[j]
                loss = left_real * right_sum[j]
                both = shared[:8] + shared[8:]
                real.append(both + (gain[:8] + gain[8:]))
                imag.append(both - (loss[:8] + loss[8:]))
        fresh = [
            [window_sums(part[k : k + 8], rows) * scale for k in range(0, slots * slots, 8)]
            for part in (real, imag)
        ]
        if total is None:
            total = fresh
        else:
            total = [[t + n for t, n in zip(ts, ns)] for ts, ns in zip(total, fresh)]
        stacked.append([jnp.concatenate(part, axis=0).astype(jnp.bfloat16) for part in total])
    return stacked


def cross_kernel(sources, late, aliased, pairs_ref, inverse_ref, *refs):
    block_refs, refs = refs[: len(sources)], refs[len(sources) + aliased :]
    if late:
        table_ref, out_ref, blocks_ref, held_ref, sem = refs
        share_refs = ()
        fetch = pltpu.make_async_copy(table_ref, held_ref, sem)
        fetch.start()
    else:
        out_ref, blocks_ref, *share_refs = refs
    block_count, _, days, slots, _, bins = blocks_ref.shape
    rounds, pairs = pairs_ref.shape[0], pairs_ref.shape[1]
    rows = lax.broadcasted_iota(jnp.int32, (8, bins), 0)
    held = days * pairs // block_count
    me = lax.axis_index("sta")
    for ref, source in zip(block_refs, sources):
        if source is None:

            def widen(n, carry):
                blocks_ref[n] = ref[n].astype(jnp.float32)
                return carry

            lax.fori_loop(0, block_count, widen, 0)
        else:
            blocks_ref[me ^ source] = ref[...].astype(jnp.float32)

    def one_pair(index, carry):
        r, p = index // pairs, index % pairs
        a, b = pairs_ref[r, p, 0], pairs_ref[r, p, 1]

        def work():
            stacked = pair_stack(a, b, inverse_ref, blocks_ref, rows)
            for d in range(days):
                row = pl.multiple_of((r * held + d % held) * slots * slots, 16)
                for c in range(2):
                    out_ref[(p * days + d) // held, c, pl.ds(row, slots * slots), :] = stacked[d][c]

        if len(late) == 0 and aliased == 0:
            work()
        else:
            waits = [(x ^ me) == away for x in (a, b) for away in late or sources]
            waits = functools.reduce(jnp.logical_or, waits)
            pl.when(jnp.logical_not(waits) if late else waits)(work)
        return carry

    lax.fori_loop(0, rounds * pairs, one_pair, 0)
    for share_ref, away in zip(share_refs, (0,) + ORDER):
        share_ref[...] = out_ref[me ^ away]
    if late:
        fetch.wait()


def cross(blocks, sources, inverse, pair_table, devices, late=(), started=(), table=None):
    parts, days, slots, windows, bins = blocks[0].shape[-5:]
    rounds, pairs, _ = pair_table.shape
    held = days * pairs // devices
    share = len(sources) / devices
    stack = rounds * held * slots * slots
    spread = devices if started else 0
    tables = [] if table is None else [table]
    wide = 4 * devices * parts * days * slots * windows * max(bins, 128)
    work = int(rounds * pairs * days * slots * slots * windows * bins * share)
    return pl.pallas_call(
        functools.partial(cross_kernel, sources, late, len(started)),
        in_specs=[pl.BlockSpec(memory_space=pltpu.SMEM)] * 2
        + [pl.BlockSpec(memory_space=pltpu.VMEM)] * (len(blocks) + len(started))
        + [pl.BlockSpec(memory_space=pl.ANY)] * len(tables),
        out_specs=[pl.BlockSpec(memory_space=pltpu.VMEM)] * (2 + spread + len(tables)),
        out_shape=[
            jax.ShapeDtypeStruct((devices, parts, stack, bins), jnp.bfloat16),
            jax.ShapeDtypeStruct((devices, parts, days, slots, windows, bins), jnp.float32),
        ]
        + [jax.ShapeDtypeStruct((parts, stack, bins), jnp.bfloat16)] * spread
        + [jax.ShapeDtypeStruct(table.shape, table.dtype) for table in tables],
        scratch_shapes=[pltpu.SemaphoreType.DMA] * len(tables),
        input_output_aliases={2 + len(blocks) + n: n for n in range(len(started))},
        compiler_params=pltpu.CompilerParams(vmem_limit_bytes=38 * MIB if late else wide + 20 * MIB),
        cost_estimate=pl.CostEstimate(
            flops=16 * work, bytes_accessed=4 << 20, transcendentals=0
        ),
        name="cross_rest" if started else "cross",
    )(pair_table, inverse, *blocks, *started, *tables)


def lag_kernel(scale, sources, *refs):
    stacked_refs, refs = refs[: len(sources)], refs[len(sources) :]
    table_ref, out_ref, left_ref, lagged_ref, out_sems = refs
    tiles, _, depth, tile = table_ref.shape
    parts, rows, _ = left_ref.shape
    half = tiles * tile
    for stacked_ref, source in zip(stacked_refs, sources):
        bins = stacked_ref.shape[-1]
        if source is None:
            for src in range(stacked_ref.shape[0]):
                for c in range(parts):
                    left_ref[c, :, src * bins : (src + 1) * bins] = stacked_ref[src, c]
        else:
            at = pl.multiple_of((lax.axis_index("sta") ^ source) * bins, 128)
            for c in range(parts):
                left_ref[c, :, pl.ds(at, bins)] = stacked_ref[c]

    turn = lax.broadcasted_iota(jnp.int32, (depth, 128), 0) % 4
    cosine = jnp.where(turn == 0, 1.0, jnp.where(turn == 2, -1.0, 0.0)).astype(jnp.bfloat16)
    sine = jnp.where(turn == 1, 1.0, jnp.where(turn == 3, -1.0, 0.0)).astype(jnp.bfloat16)
    before = jnp.dot(left_ref[0], cosine, preferred_element_type=jnp.float32)
    before = (before + jnp.dot(left_ref[1], sine, preferred_element_type=jnp.float32)) * scale

    lane = lax.broadcasted_iota(jnp.int32, (rows, 128), 1)
    flip = (128 - lane) % 128
    stores = []
    for t in reversed(range(tiles)):
        even = jnp.dot(left_ref[0], table_ref[t, 0], preferred_element_type=jnp.float32) * scale
        odd = jnp.dot(left_ref[1], table_ref[t, 1], preferred_element_type=jnp.float32) * scale
        lagged_ref[:, half + t * tile : half + (t + 1) * tile] = even + odd
        gap = even - odd
        for sub in reversed(range(tile // 128)):
            turned = jnp.take_along_axis(gap[:, sub * 128 : (sub + 1) * 128], flip, axis=1)
            at = half - t * tile - (sub + 1) * 128
            lagged_ref[:, at : at + 128] = jnp.where(lane == 0, before, turned)
            before = turned
        for k, at in enumerate((half + t * tile, half - (t + 1) * tile)):
            stores.append(
                pltpu.make_async_copy(
                    lagged_ref.at[:, at : at + tile],
                    out_ref.at[:, at : at + tile],
                    out_sems.at[2 * t + k],
                )
            )
            stores[-1].start()
    for store in stores:
        store.wait()


def lags(stacked, sources, table, scale):
    parts, rows, _ = stacked[0].shape[-3:]
    tiles, _, depth, tile = table.shape
    lag_count = 2 * tiles * tile
    return pl.pallas_call(
        functools.partial(lag_kernel, scale, sources),
        in_specs=[pl.BlockSpec(memory_space=pltpu.VMEM)] * (len(stacked) + 1),
        out_specs=pl.BlockSpec(memory_space=pl.ANY),
        out_shape=jax.ShapeDtypeStruct((rows, lag_count), jnp.float32),
        scratch_shapes=[
            pltpu.VMEM((parts, rows, depth), jnp.bfloat16),
            pltpu.VMEM((rows, lag_count), jnp.float32),
            pltpu.SemaphoreType.DMA((2 * tiles,)),
        ],
        compiler_params=pltpu.CompilerParams(vmem_limit_bytes=20 * MIB),
        name="lags",
    )(*stacked, table)


def swap(shares, sources, devices):
    received = []
    sent = []
    for share, away in zip(shares, sources):
        if away:
            if len(sent) >= 5:
                share, _ = lax.optimization_barrier((share, sent[-5]))
            share = lax.ppermute(share, "sta", [(n, n ^ away) for n in range(devices)])
            sent.append(share)
        received.append(share)
    return received


def local(table, spectra, block_counts, window_masks, pair_table):
    devices = lax.axis_size("sta")
    parts, days, windows, slots, total = spectra.shape
    rounds, pairs, _ = pair_table.shape
    held = days * pairs // devices
    if devices == len(ORDER) + 1 and total % (128 * devices) == 0:
        sources = ORDER + (0,)
        shares = pieces(spectra, block_counts, window_masks, devices, sources[:FIRST], "pack_first")
        shares += pieces(spectra, block_counts, window_masks, devices, sources[FIRST:], "pack_rest")
        blocks = swap(shares, sources, devices)
    else:
        packed = pack(spectra, block_counts, window_masks, devices)
        sources = (None,)
        blocks = [lax.all_to_all(packed, "sta", split_axis=0, concat_axis=0, tiled=True)]
    weights = window_masks.astype(jnp.float32)
    joint = jnp.einsum("dwa,dwb->dab", weights, weights)
    inverse = (1.0 / jnp.maximum(joint, 1.0)).reshape(-1)
    if len(sources) > 1:
        late = sources[-1 - LATE : -1]
        soon = [n for n, away in enumerate(sources) if away not in late]
        *started, table = cross(
            [blocks[n] for n in soon],
            tuple(sources[n] for n in soon),
            inverse,
            pair_table,
            devices,
            late,
            table=table,
        )
        shares = cross(
            blocks[-1 - LATE : -1], late, inverse, pair_table, devices, (), tuple(started)
        )[2:]
        sources = (0,) + ORDER
        received = swap(shares, sources, devices)
    else:
        stacked, _ = cross(blocks, sources, inverse, pair_table, devices)
        received = [lax.all_to_all(stacked, "sta", split_axis=0, concat_axis=0, tiled=True)]
    lagged = lags(received, sources, table, 1.0 / math.sqrt(total))
    return lagged.reshape(rounds, held, slots * slots, LAGS)


def solution(mesh):
    placed = (P(None, "grp", None, "sta", None), P(), P("grp", None, None), P())

    def run(spectra, block_counts, window_masks, pair_table):
        table = phase_tiles(spectra.shape[-1], LAGS, 256)
        return jax.shard_map(
            functools.partial(local, table),
            mesh=mesh,
            in_specs=placed,
            out_specs=P("grp", "sta", None, None),
            check_vma=False,
        )(spectra, block_counts, window_masks, pair_table)

    return run
```

```python
import functools
import math

import jax
import jax.numpy as jnp
import ml_dtypes
import numpy as np
from jax import lax
from jax.experimental import pallas as pl
from jax.experimental.pallas import tpu as pltpu
from jax.sharding import PartitionSpec as P

LAGS = 2048
MIB = 1 << 20
ORDER = (12, 1, 13, 2, 14, 3, 15, 4, 8, 5, 9, 6, 10, 7, 11)
FIRST = 3
LATE = 3


def phase_tiles(freq_count, lag_count, tile):
    freqs = np.arange(freq_count, dtype=np.int64)
    shifts = np.arange(lag_count // 2, dtype=np.int64)
    phases = np.mod(freqs[:, None] * shifts[None, :], 2 * freq_count)
    angles = np.arange(2 * freq_count) * (math.pi / freq_count)
    cosines = np.cos(angles).astype(np.float32).astype(ml_dtypes.bfloat16)[phases]
    sines = (-np.sin(angles)).astype(np.float32).astype(ml_dtypes.bfloat16)[phases]
    both = np.stack([cosines, sines]).reshape(2, freq_count, -1, tile)
    return np.ascontiguousarray(both.transpose(2, 0, 1, 3))


def pack_kernel(
    devices, counts_ref, masks_ref, spectra_ref, out_ref, raw_ref, rows_ref, ready_ref, in_sems, out_sems
):
    me = lax.axis_index("sta")
    parts, days, windows, slots, _ = spectra_ref.shape
    bins = out_ref.shape[-1]
    count = counts_ref[me]

    def load(step):
        c, d = step // days, step % days
        return pltpu.make_async_copy(spectra_ref.at[c, d], raw_ref.at[c, d], in_sems.at[step])

    def store(step):
        c, d = step // days, step % days
        return pltpu.make_async_copy(ready_ref.at[:, c, d], out_ref.at[:, c, d], out_sems.at[step])

    for step in range(parts * days):
        load(step).start()
    lane = lax.broadcasted_iota(jnp.int32, masks_ref.shape[1:], 1)

    def one(step, carry):
        c, d = step // days, step % days
        mine = jnp.where(lane == me, masks_ref[d], 0)
        keep = (jnp.sum(mine, axis=1, keepdims=True) > 0).astype(jnp.float32)
        load(step).wait()
        for owner in range(devices):
            for w in range(windows):
                rows_ref[owner, w * slots : (w + 1) * slots, :] = raw_ref[
                    c, d, w, :, owner * bins : (owner + 1) * bins
                ].astype(jnp.float32)
        for slot in range(slots):
            live = keep * jnp.where(slot < count, 1.0, 0.0)
            wide = jnp.broadcast_to(live, (windows, bins))
            for owner in range(devices):
                picked = rows_ref[owner, pl.ds(slot, windows, stride=slots), :]
                ready_ref[owner, c, d, slot] = (picked * wide).astype(jnp.bfloat16)
        store(step).start()
        return carry

    lax.fori_loop(0, parts * days, one, 0)
    for step in range(parts * days):
        store(step).wait()


def piece_kernel(aways, counts_ref, masks_ref, spectra_ref, *refs):
    out_refs, raw_ref, rows_ref, sems = refs[: len(aways)], refs[-3], refs[-2], refs[-1]
    me = lax.axis_index("sta")
    parts, days, windows, slots, bins = raw_ref.shape[1:]
    count = counts_ref[me]
    loads = []
    for n, away in enumerate(aways):
        columns = pl.ds(pl.multiple_of((me ^ away) * bins, 128), bins)
        loads.append(
            pltpu.make_async_copy(spectra_ref.at[:, :, :, :, columns], raw_ref.at[n], sems.at[n])
        )
        loads[n].start()
    lane = lax.broadcasted_iota(jnp.int32, masks_ref.shape[1:], 1)
    wide = []
    for d in range(days):
        mine = jnp.where(lane == me, masks_ref[d], 0)
        keep = (jnp.sum(mine, axis=1, keepdims=True) > 0).astype(jnp.float32)
        wide.append(jnp.broadcast_to(keep, (windows, bins)))
    live = [jnp.where(slot < count, 1.0, 0.0) for slot in range(slots)]
    for n, out_ref in enumerate(out_refs):
        loads[n].wait()

        def one(c, carry):
            for d in range(days):
                for w in range(windows):
                    rows_ref[d, w * slots : (w + 1) * slots, :] = raw_ref[n, c, d, w].astype(
                        jnp.float32
                    )
                for slot in range(slots):
                    picked = rows_ref[d, pl.ds(slot, windows, stride=slots), :]
                    out_ref[c, d, slot] = (picked * (wide[d] * live[slot])).astype(jnp.bfloat16)
            return carry

        lax.fori_loop(0, parts, one, 0)


def pieces(spectra, block_counts, window_masks, devices, aways, name):
    parts, days, windows, slots, total = spectra.shape
    bins = total // devices
    share = jax.ShapeDtypeStruct((parts, days, slots, windows, bins), jnp.bfloat16)
    return pl.pallas_call(
        functools.partial(piece_kernel, aways),
        in_specs=[
            pl.BlockSpec(memory_space=pltpu.SMEM),
            pl.BlockSpec(memory_space=pltpu.VMEM),
            pl.BlockSpec(memory_space=pl.ANY),
        ],
        out_specs=[pl.BlockSpec(memory_space=pltpu.VMEM)] * len(aways),
        out_shape=[share] * len(aways),
        scratch_shapes=[
            pltpu.VMEM((len(aways), parts, days, windows, slots, bins), jnp.bfloat16),
            pltpu.VMEM((days, windows * slots, bins), jnp.float32),
            pltpu.SemaphoreType.DMA((len(aways),)),
        ],
        compiler_params=pltpu.CompilerParams(vmem_limit_bytes=60 * MIB),
        name=name,
    )(block_counts, window_masks, spectra)


def pack(spectra, block_counts, window_masks, devices):
    parts, days, windows, slots, total = spectra.shape
    bins = total // devices
    packed = (devices, parts, days, slots, windows, bins)
    return pl.pallas_call(
        functools.partial(pack_kernel, devices),
        in_specs=[
            pl.BlockSpec(memory_space=pltpu.SMEM),
            pl.BlockSpec(memory_space=pltpu.VMEM),
            pl.BlockSpec(memory_space=pl.ANY),
        ],
        out_specs=pl.BlockSpec(memory_space=pl.ANY),
        out_shape=jax.ShapeDtypeStruct(packed, jnp.bfloat16),
        scratch_shapes=[
            pltpu.VMEM(spectra.shape, jnp.bfloat16),
            pltpu.VMEM((devices, windows * slots, bins), jnp.float32),
            pltpu.VMEM(packed, jnp.bfloat16),
            pltpu.SemaphoreType.DMA((parts * days,)),
            pltpu.SemaphoreType.DMA((parts * days,)),
        ],
        compiler_params=pltpu.CompilerParams(vmem_limit_bytes=60 * MIB),
        name="pack",
    )(block_counts, window_masks, spectra)


def window_sums(terms, rows):
    for step in (1, 2, 4):
        own = (rows & step) == 0
        terms = [
            jnp.where(own, first, second) + pltpu.roll(jnp.where(own, second, first), 8 - step, 0)
            for first, second in zip(terms[::2], terms[1::2])
        ]
    return terms[0]


def pair_stack(a, b, inverse_ref, blocks_ref, rows):
    block_count, _, days, slots = blocks_ref.shape[:4]
    total = None
    stacked = []
    for d in range(days):
        scale = inverse_ref[(d * block_count + a) * block_count + b]
        right = [[blocks_ref[b, c, d, s].astype(jnp.float32) for s in range(slots)] for c in range(2)]
        right_sum = [x + y for x, y in zip(right[0], right[1])]
        right_gap = [y - x for x, y in zip(right[0], right[1])]
        real, imag = [], []
        for i in range(slots):
            left_real = blocks_ref[a, 0, d, i].astype(jnp.float32)
            left_imag = blocks_ref[a, 1, d, i].astype(jnp.float32)
            left_sum = left_real + left_imag
            for j in range(slots):
                shared = left_sum * right[0][j]
                gain = left_imag * right_gap[j]
                loss = left_real * right_sum[j]
                both = shared[:8] + shared[8:]
                real.append(both + (gain[:8] + gain[8:]))
                imag.append(both - (loss[:8] + loss[8:]))
        fresh = [
            [window_sums(part[k : k + 8], rows) * scale for k in range(0, slots * slots, 8)]
            for part in (real, imag)
        ]
        if total is None:
            total = fresh
        else:
            total = [[t + n for t, n in zip(ts, ns)] for ts, ns in zip(total, fresh)]
        stacked.append([jnp.concatenate(part, axis=0).astype(jnp.bfloat16) for part in total])
    return stacked


def cross_kernel(sources, late, aliased, pairs_ref, inverse_ref, *refs):
    block_refs, refs = refs[: len(sources)], refs[len(sources) + aliased :]
    if late:
        table_ref, out_ref, blocks_ref, held_ref, sem = refs
        share_refs = ()
        fetch = pltpu.make_async_copy(table_ref, held_ref, sem)
        fetch.start()
    else:
        out_ref, blocks_ref, *share_refs = refs
    block_count, _, days, slots, _, bins = blocks_ref.shape
    rounds, pairs = pairs_ref.shape[0], pairs_ref.shape[1]
    rows = lax.broadcasted_iota(jnp.int32, (8, bins), 0)
    held = days * pairs // block_count
    me = lax.axis_index("sta")
    for ref, source in zip(block_refs, sources):
        if source is None:

            def widen(n, carry):
                blocks_ref[n] = ref[n].astype(jnp.float32)
                return carry

            lax.fori_loop(0, block_count, widen, 0)
        else:
            blocks_ref[me ^ source] = ref[...].astype(jnp.float32)

    def one_pair(index, carry):
        r, p = index // pairs, index % pairs
        a, b = pairs_ref[r, p, 0], pairs_ref[r, p, 1]

        def work():
            stacked = pair_stack(a, b, inverse_ref, blocks_ref, rows)
            for d in range(days):
                row = pl.multiple_of((r * held + d % held) * slots * slots, 16)
                for c in range(2):
                    out_ref[(p * days + d) // held, c, pl.ds(row, slots * slots), :] = stacked[d][c]

        if len(late) == 0 and aliased == 0:
            work()
        else:
            waits = [(x ^ me) == away for x in (a, b) for away in late or sources]
            waits = functools.reduce(jnp.logical_or, waits)
            pl.when(jnp.logical_not(waits) if late else waits)(work)
        return carry

    lax.fori_loop(0, rounds * pairs, one_pair, 0)
    for share_ref, away in zip(share_refs, (0,) + ORDER):
        share_ref[...] = out_ref[me ^ away]
    if late:
        fetch.wait()


def cross(blocks, sources, inverse, pair_table, devices, late=(), started=(), table=None):
    parts, days, slots, windows, bins = blocks[0].shape[-5:]
    rounds, pairs, _ = pair_table.shape
    held = days * pairs // devices
    share = len(sources) / devices
    stack = rounds * held * slots * slots
    spread = devices if started else 0
    tables = [] if table is None else [table]
    wide = 4 * devices * parts * days * slots * windows * max(bins, 128)
    work = int(rounds * pairs * days * slots * slots * windows * bins * share)
    return pl.pallas_call(
        functools.partial(cross_kernel, sources, late, len(started)),
        in_specs=[pl.BlockSpec(memory_space=pltpu.SMEM)] * 2
        + [pl.BlockSpec(memory_space=pltpu.VMEM)] * (len(blocks) + len(started))
        + [pl.BlockSpec(memory_space=pl.ANY)] * len(tables),
        out_specs=[pl.BlockSpec(memory_space=pltpu.VMEM)] * (2 + spread + len(tables)),
        out_shape=[
            jax.ShapeDtypeStruct((devices, parts, stack, bins), jnp.bfloat16),
            jax.ShapeDtypeStruct((devices, parts, days, slots, windows, bins), jnp.float32),
        ]
        + [jax.ShapeDtypeStruct((parts, stack, bins), jnp.bfloat16)] * spread
        + [jax.ShapeDtypeStruct(table.shape, table.dtype) for table in tables],
        scratch_shapes=[pltpu.SemaphoreType.DMA] * len(tables),
        input_output_aliases={2 + len(blocks) + n: n for n in range(len(started))},
        compiler_params=pltpu.CompilerParams(vmem_limit_bytes=38 * MIB if late else wide + 20 * MIB),
        cost_estimate=pl.CostEstimate(
            flops=16 * work, bytes_accessed=4 << 20, transcendentals=0
        ),
        name="cross_rest" if started else "cross",
    )(pair_table, inverse, *blocks, *started, *tables)


def quarter_turns(depth):
    turn = lax.broadcasted_iota(jnp.int32, (depth, 128), 0) % 4
    cosine = jnp.where(turn == 0, 1.0, jnp.where(turn == 2, -1.0, 0.0))
    sine = jnp.where(turn == 1, 1.0, jnp.where(turn == 3, -1.0, 0.0))
    return cosine.astype(jnp.bfloat16), sine.astype(jnp.bfloat16)


def product(left, right):
    return jnp.dot(left, right, preferred_element_type=jnp.float32)


def write_lags(scale, sums, before, out_ref, lagged_ref, out_sems):
    rows, lag_count = lagged_ref.shape
    tiles = out_sems.shape[0] // 2
    half = lag_count // 2
    tile = half // tiles
    lane = lax.broadcasted_iota(jnp.int32, (rows, 128), 1)
    flip = (128 - lane) % 128
    before = before * scale
    stores = []
    for t in reversed(range(tiles)):
        even, odd = sums(t)
        even, odd = even * scale, odd * scale
        lagged_ref[:, half + t * tile : half + (t + 1) * tile] = even + odd
        gap = even - odd
        for sub in reversed(range(tile // 128)):
            turned = jnp.take_along_axis(gap[:, sub * 128 : (sub + 1) * 128], flip, axis=1)
            at = half - t * tile - (sub + 1) * 128
            lagged_ref[:, at : at + 128] = jnp.where(lane == 0, before, turned)
            before = turned
        for k, at in enumerate((half + t * tile, half - (t + 1) * tile)):
            stores.append(
                pltpu.make_async_copy(
                    lagged_ref.at[:, at : at + tile],
                    out_ref.at[:, at : at + tile],
                    out_sems.at[2 * t + k],
                )
            )
            stores[-1].start()
    for store in stores:
        store.wait()


def place(source, bins):
    return pl.ds(pl.multiple_of((lax.axis_index("sta") ^ source) * bins, 128), bins)


def lag_kernel(scale, sources, late, *refs):
    stacked_refs, table_ref, refs = refs[: len(sources)], refs[len(sources)], refs[len(sources) + 1 :]
    tiles, parts, depth, tile = table_ref.shape
    left_ref = refs[2]
    rows = left_ref.shape[1]
    for stacked_ref, source in zip(stacked_refs, sources):
        bins = stacked_ref.shape[-1]
        for c in range(parts):
            if source is None:
                for src in range(stacked_ref.shape[0]):
                    left_ref[c, :, src * bins : (src + 1) * bins] = stacked_ref[src, c]
            else:
                left_ref[c, :, place(source, bins)] = stacked_ref[c]
    for source in late:
        for c in range(parts):
            left_ref[c, :, place(source, bins)] = jnp.zeros((rows, bins), jnp.bfloat16)

    cosine, sine = quarter_turns(depth)
    before = product(left_ref[0], cosine) + product(left_ref[1], sine)

    def sums(t):
        return product(left_ref[0], table_ref[t, 0]), product(left_ref[1], table_ref[t, 1])

    if late:
        sums_ref, before_ref, _ = refs
        before_ref[...] = before
        for t in range(tiles):
            sums_ref[t, 0], sums_ref[t, 1] = sums(t)
    else:
        out_ref, lagged_ref, _, out_sems = refs
        write_lags(scale, sums, before, out_ref, lagged_ref, out_sems)


def rest_kernel(scale, sources, *refs):
    stacked_refs, refs = refs[: len(sources)], refs[len(sources) :]
    table_ref, sums_ref, before_ref, out_ref, lagged_ref, out_sems = refs
    bins = stacked_refs[0].shape[-1]
    cosine, sine = quarter_turns(bins)
    before = before_ref[...]
    for ref in stacked_refs:
        before = before + (product(ref[0], cosine) + product(ref[1], sine))

    def sums(t):
        totals = []
        for c in range(2):
            total = sums_ref[t, c]
            for ref, source in zip(stacked_refs, sources):
                total = total + product(ref[c], table_ref[t, c, place(source, bins), :])
            totals.append(total)
        return totals

    write_lags(scale, sums, before, out_ref, lagged_ref, out_sems)


def lags(stacked, sources, table, scale, late=(), started=()):
    parts, rows, _ = stacked[0].shape[-3:]
    tiles, _, depth, tile = table.shape
    lag_count = 2 * tiles * tile
    vmem = pl.BlockSpec(memory_space=pltpu.VMEM)
    left = pltpu.VMEM((parts, rows, depth), jnp.bfloat16)
    if late:
        body = functools.partial(lag_kernel, scale, sources, late)
        out_specs = [vmem] * 2
        out_shape = [
            jax.ShapeDtypeStruct((tiles, parts, rows, tile), jnp.float32),
            jax.ShapeDtypeStruct((rows, 128), jnp.float32),
        ]
        scratch = [left]
    else:
        out_specs = pl.BlockSpec(memory_space=pl.ANY)
        out_shape = jax.ShapeDtypeStruct((rows, lag_count), jnp.float32)
        scratch = [pltpu.VMEM((rows, lag_count), jnp.float32)]
        if started:
            body = functools.partial(rest_kernel, scale, sources)
        else:
            body = functools.partial(lag_kernel, scale, sources, late)
            scratch.append(left)
        scratch.append(pltpu.SemaphoreType.DMA((2 * tiles,)))
    return pl.pallas_call(
        body,
        in_specs=[vmem] * (len(stacked) + 1 + len(started)),
        out_specs=out_specs,
        out_shape=out_shape,
        scratch_shapes=scratch,
        compiler_params=pltpu.CompilerParams(vmem_limit_bytes=20 * MIB),
        cost_estimate=pl.CostEstimate(
            flops=2 * rows * depth * lag_count, bytes_accessed=4 << 20, transcendentals=0
        ),
        name="lags_first" if late else "lags",
    )(*stacked, table, *started)


def swap(shares, sources, devices):
    received = []
    sent = []
    for share, away in zip(shares, sources):
        if away:
            if len(sent) >= 5:
                share, _ = lax.optimization_barrier((share, sent[-5]))
            share = lax.ppermute(share, "sta", [(n, n ^ away) for n in range(devices)])
            sent.append(share)
        received.append(share)
    return received


def local(table, spectra, block_counts, window_masks, pair_table):
    devices = lax.axis_size("sta")
    parts, days, windows, slots, total = spectra.shape
    rounds, pairs, _ = pair_table.shape
    held = days * pairs // devices
    if devices == len(ORDER) + 1 and total % (128 * devices) == 0:
        sources = ORDER + (0,)
        shares = pieces(spectra, block_counts, window_masks, devices, sources[:FIRST], "pack_first")
        shares += pieces(spectra, block_counts, window_masks, devices, sources[FIRST:], "pack_rest")
        blocks = swap(shares, sources, devices)
    else:
        packed = pack(spectra, block_counts, window_masks, devices)
        sources = (None,)
        blocks = [lax.all_to_all(packed, "sta", split_axis=0, concat_axis=0, tiled=True)]
    weights = window_masks.astype(jnp.float32)
    joint = jnp.einsum("dwa,dwb->dab", weights, weights)
    inverse = (1.0 / jnp.maximum(joint, 1.0)).reshape(-1)
    if len(sources) > 1:
        late = sources[-1 - LATE : -1]
        soon = [n for n, away in enumerate(sources) if away not in late]
        *started, table = cross(
            [blocks[n] for n in soon],
            tuple(sources[n] for n in soon),
            inverse,
            pair_table,
            devices,
            late,
            table=table,
        )
        shares = cross(
            blocks[-1 - LATE : -1], late, inverse, pair_table, devices, (), tuple(started)
        )[2:]
        sources = (0,) + ORDER
        received = swap(shares, sources, devices)
    else:
        stacked, _ = cross(blocks, sources, inverse, pair_table, devices)
        received = [lax.all_to_all(stacked, "sta", split_axis=0, concat_axis=0, tiled=True)]
    scale = 1.0 / math.sqrt(total)
    if len(sources) > 1:
        kept = len(sources) - LATE
        started = lags(received[:kept], sources[:kept], table, scale, sources[kept:])
        lagged = lags(received[kept:], sources[kept:], table, scale, (), tuple(started))
    else:
        lagged = lags(received, sources, table, scale)
    return lagged.reshape(rounds, held, slots * slots, LAGS)


def solution(mesh):
    placed = (P(None, "grp", None, "sta", None), P(), P("grp", None, None), P())

    def run(spectra, block_counts, window_masks, pair_table):
        table = phase_tiles(spectra.shape[-1], LAGS, 256)
        return jax.shard_map(
            functools.partial(local, table),
            mesh=mesh,
            in_specs=placed,
            out_specs=P("grp", "sta", None, None),
            check_vma=False,
        )(spectra, block_counts, window_masks, pair_table)

    return run
```

```python
import functools
import math

import jax
import jax.numpy as jnp
import ml_dtypes
import numpy as np
from jax import lax
from jax.experimental import pallas as pl
from jax.experimental.pallas import tpu as pltpu
from jax.sharding import PartitionSpec as P

LAGS = 2048
MIB = 1 << 20
ORDER = (12, 1, 13, 2, 14, 3, 15, 4, 8, 5, 9, 6, 10, 7, 11)
FIRST = 2
LATE = 3


def phase_tiles(freq_count, lag_count, tile):
    freqs = np.arange(freq_count, dtype=np.int64)
    shifts = np.arange(lag_count // 2, dtype=np.int64)
    phases = np.mod(freqs[:, None] * shifts[None, :], 2 * freq_count)
    angles = np.arange(2 * freq_count) * (math.pi / freq_count)
    cosines = np.cos(angles).astype(np.float32).astype(ml_dtypes.bfloat16)[phases]
    sines = (-np.sin(angles)).astype(np.float32).astype(ml_dtypes.bfloat16)[phases]
    both = np.stack([cosines, sines]).reshape(2, freq_count, -1, tile)
    return np.ascontiguousarray(both.transpose(2, 0, 1, 3))


def pack_kernel(
    devices, counts_ref, masks_ref, spectra_ref, out_ref, raw_ref, rows_ref, ready_ref, in_sems, out_sems
):
    me = lax.axis_index("sta")
    parts, days, windows, slots, _ = spectra_ref.shape
    bins = out_ref.shape[-1]
    count = counts_ref[me]

    def load(step):
        c, d = step // days, step % days
        return pltpu.make_async_copy(spectra_ref.at[c, d], raw_ref.at[c, d], in_sems.at[step])

    def store(step):
        c, d = step // days, step % days
        return pltpu.make_async_copy(ready_ref.at[:, c, d], out_ref.at[:, c, d], out_sems.at[step])

    for step in range(parts * days):
        load(step).start()
    lane = lax.broadcasted_iota(jnp.int32, masks_ref.shape[1:], 1)

    def one(step, carry):
        c, d = step // days, step % days
        mine = jnp.where(lane == me, masks_ref[d], 0)
        keep = (jnp.sum(mine, axis=1, keepdims=True) > 0).astype(jnp.float32)
        load(step).wait()
        for owner in range(devices):
            for w in range(windows):
                rows_ref[owner, w * slots : (w + 1) * slots, :] = raw_ref[
                    c, d, w, :, owner * bins : (owner + 1) * bins
                ].astype(jnp.float32)
        for slot in range(slots):
            live = keep * jnp.where(slot < count, 1.0, 0.0)
            wide = jnp.broadcast_to(live, (windows, bins))
            for owner in range(devices):
                picked = rows_ref[owner, pl.ds(slot, windows, stride=slots), :]
                ready_ref[owner, c, d, slot] = (picked * wide).astype(jnp.bfloat16)
        store(step).start()
        return carry

    lax.fori_loop(0, parts * days, one, 0)
    for step in range(parts * days):
        store(step).wait()


def piece_kernel(aways, counts_ref, masks_ref, spectra_ref, *refs):
    out_refs, (raw_ref, rows_ref, held_ref, number_ref, sems) = refs[: len(aways)], refs[len(aways) :]
    me = lax.axis_index("sta")
    parts, days, windows, slots, bins = raw_ref.shape[1:]
    small = [
        pltpu.make_async_copy(counts_ref, number_ref, sems.at[len(aways)]),
        pltpu.make_async_copy(masks_ref, held_ref, sems.at[len(aways) + 1]),
    ]
    for copy in small:
        copy.start()
    loads = []
    for n, away in enumerate(aways):
        columns = pl.ds(pl.multiple_of((me ^ away) * bins, 128), bins)
        loads.append(
            pltpu.make_async_copy(spectra_ref.at[:, :, :, :, columns], raw_ref.at[n], sems.at[n])
        )
        loads[n].start()
    for copy in small:
        copy.wait()
    count = number_ref[me]
    lane = lax.broadcasted_iota(jnp.int32, masks_ref.shape[1:], 1)
    wide = []
    for d in range(days):
        mine = jnp.where(lane == me, held_ref[d], 0)
        keep = (jnp.sum(mine, axis=1, keepdims=True) > 0).astype(jnp.float32)
        wide.append(jnp.broadcast_to(keep, (windows, bins)))
    live = [jnp.where(slot < count, 1.0, 0.0) for slot in range(slots)]
    for n, out_ref in enumerate(out_refs):
        loads[n].wait()

        def one(c, carry):
            for d in range(days):
                for w in range(windows):
                    rows_ref[d, w * slots : (w + 1) * slots, :] = raw_ref[n, c, d, w].astype(
                        jnp.float32
                    )
                for slot in range(slots):
                    picked = rows_ref[d, pl.ds(slot, windows, stride=slots), :]
                    out_ref[c, d, slot] = (picked * (wide[d] * live[slot])).astype(jnp.bfloat16)
            return carry

        lax.fori_loop(0, parts, one, 0)


def pieces(spectra, block_counts, window_masks, devices, aways, name):
    parts, days, windows, slots, total = spectra.shape
    bins = total // devices
    share = jax.ShapeDtypeStruct((parts, days, slots, windows, bins), jnp.bfloat16)
    return pl.pallas_call(
        functools.partial(piece_kernel, aways),
        in_specs=[
            pl.BlockSpec(memory_space=pl.ANY),
            pl.BlockSpec(memory_space=pl.ANY),
            pl.BlockSpec(memory_space=pl.ANY),
        ],
        out_specs=[pl.BlockSpec(memory_space=pltpu.VMEM)] * len(aways),
        out_shape=[share] * len(aways),
        scratch_shapes=[
            pltpu.VMEM((len(aways), parts, days, windows, slots, bins), jnp.bfloat16),
            pltpu.VMEM((days, windows * slots, bins), jnp.float32),
            pltpu.VMEM(window_masks.shape, jnp.int32),
            pltpu.SMEM(block_counts.shape, jnp.int32),
            pltpu.SemaphoreType.DMA((len(aways) + 2,)),
        ],
        compiler_params=pltpu.CompilerParams(vmem_limit_bytes=60 * MIB),
        name=name,
    )(block_counts, window_masks, spectra)


def pack(spectra, block_counts, window_masks, devices):
    parts, days, windows, slots, total = spectra.shape
    bins = total // devices
    packed = (devices, parts, days, slots, windows, bins)
    return pl.pallas_call(
        functools.partial(pack_kernel, devices),
        in_specs=[
            pl.BlockSpec(memory_space=pltpu.SMEM),
            pl.BlockSpec(memory_space=pltpu.VMEM),
            pl.BlockSpec(memory_space=pl.ANY),
        ],
        out_specs=pl.BlockSpec(memory_space=pl.ANY),
        out_shape=jax.ShapeDtypeStruct(packed, jnp.bfloat16),
        scratch_shapes=[
            pltpu.VMEM(spectra.shape, jnp.bfloat16),
            pltpu.VMEM((devices, windows * slots, bins), jnp.float32),
            pltpu.VMEM(packed, jnp.bfloat16),
            pltpu.SemaphoreType.DMA((parts * days,)),
            pltpu.SemaphoreType.DMA((parts * days,)),
        ],
        compiler_params=pltpu.CompilerParams(vmem_limit_bytes=60 * MIB),
        name="pack",
    )(block_counts, window_masks, spectra)


def window_sums(terms, rows):
    for step in (1, 2, 4):
        own = (rows & step) == 0
        terms = [
            jnp.where(own, first, second) + pltpu.roll(jnp.where(own, second, first), 8 - step, 0)
            for first, second in zip(terms[::2], terms[1::2])
        ]
    return terms[0]


def pair_stack(a, b, inverse_ref, blocks_ref, rows):
    block_count, _, days, slots = blocks_ref.shape[:4]
    total = None
    stacked = []
    for d in range(days):
        scale = inverse_ref[(d * block_count + a) * block_count + b]
        right = [[blocks_ref[b, c, d, s].astype(jnp.float32) for s in range(slots)] for c in range(2)]
        right_sum = [x + y for x, y in zip(right[0], right[1])]
        right_gap = [y - x for x, y in zip(right[0], right[1])]
        real, imag = [], []
        for i in range(slots):
            left_real = blocks_ref[a, 0, d, i].astype(jnp.float32)
            left_imag = blocks_ref[a, 1, d, i].astype(jnp.float32)
            left_sum = left_real + left_imag
            for j in range(slots):
                shared = left_sum * right[0][j]
                gain = left_imag * right_gap[j]
                loss = left_real * right_sum[j]
                both = shared[:8] + shared[8:]
                real.append(both + (gain[:8] + gain[8:]))
                imag.append(both - (loss[:8] + loss[8:]))
        fresh = [
            [window_sums(part[k : k + 8], rows) * scale for k in range(0, slots * slots, 8)]
            for part in (real, imag)
        ]
        if total is None:
            total = fresh
        else:
            total = [[t + n for t, n in zip(ts, ns)] for ts, ns in zip(total, fresh)]
        stacked.append([jnp.concatenate(part, axis=0).astype(jnp.bfloat16) for part in total])
    return stacked


def cross_kernel(sources, late, aliased, rounds, pairs, pairs_ref, inverse_ref, *refs):
    block_refs, refs = refs[: len(sources)], refs[len(sources) + aliased :]
    if late:
        table_ref, out_ref, blocks_ref, held_ref, sem = refs
        share_refs = ()
        fetch = pltpu.make_async_copy(table_ref, held_ref, sem)
        fetch.start()
    else:
        out_ref, blocks_ref, *share_refs = refs
    block_count, _, days, slots, _, bins = blocks_ref.shape
    rows = lax.broadcasted_iota(jnp.int32, (8, bins), 0)
    held = days * pairs // block_count
    me = lax.axis_index("sta")
    for ref, source in zip(block_refs, sources):
        if source is None:

            def widen(n, carry):
                blocks_ref[n] = ref[n].astype(jnp.float32)
                return carry

            lax.fori_loop(0, block_count, widen, 0)
        else:
            blocks_ref[me ^ source] = ref[...].astype(jnp.float32)

    def one_pair(r, p):
        a = pairs_ref[(r * pairs + p) * 2]
        b = pairs_ref[(r * pairs + p) * 2 + 1]

        def work():
            stacked = pair_stack(a, b, inverse_ref, blocks_ref, rows)
            for d in range(days):
                row = pl.multiple_of((r * held + d % held) * slots * slots, 16)
                for c in range(2):
                    out_ref[(p * days + d) // held, c, pl.ds(row, slots * slots), :] = stacked[d][c]

        if late:
            waits = [(x ^ me) == away for x in (a, b) for away in late]
            pl.when(jnp.logical_not(functools.reduce(jnp.logical_or, waits)))(work)
        else:
            work()

    def any_pair(index, carry):
        one_pair(index // pairs, index % pairs)
        return carry

    def late_pairs(r, carry):
        for source in sources:
            one_pair(r, pairs_ref[(rounds * pairs) * 2 + r * block_count + (me ^ source)])
        return carry

    if aliased:
        lax.fori_loop(0, rounds, late_pairs, 0)
    else:
        lax.fori_loop(0, rounds * pairs, any_pair, 0)
    for share_ref, away in zip(share_refs, (0,) + ORDER):
        share_ref[...] = out_ref[me ^ away]
    if late:
        fetch.wait()


def cross(blocks, sources, inverse, pair_table, devices, late=(), started=(), table=None):
    parts, days, slots, windows, bins = blocks[0].shape[-5:]
    rounds, pairs, _ = pair_table.shape
    held = days * pairs // devices
    share = len(sources) / devices
    stack = rounds * held * slots * slots
    spread = devices if started else 0
    tables = [] if table is None else [table]
    blocks_of = pair_table[..., None] == jnp.arange(devices, dtype=jnp.int32)
    owner = jnp.sum(blocks_of * jnp.arange(pairs, dtype=jnp.int32)[:, None, None], axis=(1, 2))
    wide = 4 * devices * parts * days * slots * windows * max(bins, 128)
    work = int(rounds * pairs * days * slots * slots * windows * bins * share)
    return pl.pallas_call(
        functools.partial(cross_kernel, sources, late, len(started), rounds, pairs),
        in_specs=[pl.BlockSpec(memory_space=pltpu.SMEM)] * 2
        + [pl.BlockSpec(memory_space=pltpu.VMEM)] * (len(blocks) + len(started))
        + [pl.BlockSpec(memory_space=pl.ANY)] * len(tables),
        out_specs=[pl.BlockSpec(memory_space=pltpu.VMEM)] * (2 + spread + len(tables)),
        out_shape=[
            jax.ShapeDtypeStruct((devices, parts, stack, bins), jnp.bfloat16),
            jax.ShapeDtypeStruct((devices, parts, days, slots, windows, bins), jnp.float32),
        ]
        + [jax.ShapeDtypeStruct((parts, stack, bins), jnp.bfloat16)] * spread
        + [jax.ShapeDtypeStruct(table.shape, table.dtype) for table in tables],
        scratch_shapes=[pltpu.SemaphoreType.DMA] * len(tables),
        input_output_aliases={2 + len(blocks) + n: n for n in range(len(started))},
        compiler_params=pltpu.CompilerParams(vmem_limit_bytes=38 * MIB if late else wide + 20 * MIB),
        cost_estimate=pl.CostEstimate(
            flops=16 * work, bytes_accessed=4 << 20, transcendentals=0
        ),
        name="cross_rest" if started else "cross",
    )(jnp.concatenate([pair_table.reshape(-1), owner.reshape(-1)]), inverse, *blocks, *started, *tables)


def quarter_turns(depth):
    turn = lax.broadcasted_iota(jnp.int32, (depth, 128), 0) % 4
    cosine = jnp.where(turn == 0, 1.0, jnp.where(turn == 2, -1.0, 0.0))
    sine = jnp.where(turn == 1, 1.0, jnp.where(turn == 3, -1.0, 0.0))
    return cosine.astype(jnp.bfloat16), sine.astype(jnp.bfloat16)


def product(left, right):
    return jnp.dot(left, right, preferred_element_type=jnp.float32)


def write_lags(scale, sums, before, out_ref, lagged_ref, out_sems):
    rows, lag_count = lagged_ref.shape
    tiles = out_sems.shape[0] // 2
    half = lag_count // 2
    tile = half // tiles
    lane = lax.broadcasted_iota(jnp.int32, (rows, 128), 1)
    flip = (128 - lane) % 128
    before = before * scale
    stores = []
    for t in reversed(range(tiles)):
        even, odd = sums(t)
        even, odd = even * scale, odd * scale
        lagged_ref[:, half + t * tile : half + (t + 1) * tile] = even + odd
        gap = even - odd
        for sub in reversed(range(tile // 128)):
            turned = jnp.take_along_axis(gap[:, sub * 128 : (sub + 1) * 128], flip, axis=1)
            at = half - t * tile - (sub + 1) * 128
            lagged_ref[:, at : at + 128] = jnp.where(lane == 0, before, turned)
            before = turned
        for k, at in enumerate((half + t * tile, half - (t + 1) * tile)):
            stores.append(
                pltpu.make_async_copy(
                    lagged_ref.at[:, at : at + tile],
                    out_ref.at[:, at : at + tile],
                    out_sems.at[2 * t + k],
                )
            )
            stores[-1].start()
    for store in stores:
        store.wait()


def place(source, bins):
    return pl.ds(pl.multiple_of((lax.axis_index("sta") ^ source) * bins, 128), bins)


def lag_kernel(scale, sources, late, *refs):
    stacked_refs, table_ref, refs = refs[: len(sources)], refs[len(sources)], refs[len(sources) + 1 :]
    tiles, parts, depth, tile = table_ref.shape
    left_ref = refs[2]
    rows = left_ref.shape[1]
    for stacked_ref, source in zip(stacked_refs, sources):
        bins = stacked_ref.shape[-1]
        for c in range(parts):
            if source is None:
                for src in range(stacked_ref.shape[0]):
                    left_ref[c, :, src * bins : (src + 1) * bins] = stacked_ref[src, c]
            else:
                left_ref[c, :, place(source, bins)] = stacked_ref[c]
    for source in late:
        for c in range(parts):
            left_ref[c, :, place(source, bins)] = jnp.zeros((rows, bins), jnp.bfloat16)

    cosine, sine = quarter_turns(depth)
    before = product(left_ref[0], cosine) + product(left_ref[1], sine)

    def sums(t):
        return product(left_ref[0], table_ref[t, 0]), product(left_ref[1], table_ref[t, 1])

    if late:
        sums_ref, before_ref, _ = refs
        before_ref[...] = before
        for t in range(tiles):
            sums_ref[t, 0], sums_ref[t, 1] = sums(t)
    else:
        out_ref, lagged_ref, _, out_sems = refs
        write_lags(scale, sums, before, out_ref, lagged_ref, out_sems)


def rest_kernel(scale, sources, *refs):
    stacked_refs, refs = refs[: len(sources)], refs[len(sources) :]
    table_ref, sums_ref, before_ref, out_ref, lagged_ref, out_sems = refs
    bins = stacked_refs[0].shape[-1]
    cosine, sine = quarter_turns(bins)
    before = before_ref[...]
    for ref in stacked_refs:
        before = before + (product(ref[0], cosine) + product(ref[1], sine))

    def sums(t):
        totals = []
        for c in range(2):
            total = sums_ref[t, c]
            for ref, source in zip(stacked_refs, sources):
                total = total + product(ref[c], table_ref[t, c, place(source, bins), :])
            totals.append(total)
        return totals

    write_lags(scale, sums, before, out_ref, lagged_ref, out_sems)


def lags(stacked, sources, table, scale, late=(), started=()):
    parts, rows, _ = stacked[0].shape[-3:]
    tiles, _, depth, tile = table.shape
    lag_count = 2 * tiles * tile
    vmem = pl.BlockSpec(memory_space=pltpu.VMEM)
    left = pltpu.VMEM((parts, rows, depth), jnp.bfloat16)
    if late:
        body = functools.partial(lag_kernel, scale, sources, late)
        out_specs = [vmem] * 2
        out_shape = [
            jax.ShapeDtypeStruct((tiles, parts, rows, tile), jnp.float32),
            jax.ShapeDtypeStruct((rows, 128), jnp.float32),
        ]
        scratch = [left]
    else:
        out_specs = pl.BlockSpec(memory_space=pl.ANY)
        out_shape = jax.ShapeDtypeStruct((rows, lag_count), jnp.float32)
        scratch = [pltpu.VMEM((rows, lag_count), jnp.float32)]
        if started:
            body = functools.partial(rest_kernel, scale, sources)
        else:
            body = functools.partial(lag_kernel, scale, sources, late)
            scratch.append(left)
        scratch.append(pltpu.SemaphoreType.DMA((2 * tiles,)))
    return pl.pallas_call(
        body,
        in_specs=[vmem] * (len(stacked) + 1 + len(started)),
        out_specs=out_specs,
        out_shape=out_shape,
        scratch_shapes=scratch,
        compiler_params=pltpu.CompilerParams(vmem_limit_bytes=20 * MIB),
        cost_estimate=pl.CostEstimate(
            flops=2 * rows * depth * lag_count, bytes_accessed=4 << 20, transcendentals=0
        ),
        name="lags_first" if late else "lags",
    )(*stacked, table, *started)


def swap(shares, sources, devices):
    received = []
    sent = []
    for share, away in zip(shares, sources):
        if away:
            if len(sent) >= 5:
                share, _ = lax.optimization_barrier((share, sent[-5]))
            share = lax.ppermute(share, "sta", [(n, n ^ away) for n in range(devices)])
            sent.append(share)
        received.append(share)
    return received


def local(table, spectra, block_counts, window_masks, pair_table):
    devices = lax.axis_size("sta")
    parts, days, windows, slots, total = spectra.shape
    rounds, pairs, _ = pair_table.shape
    held = days * pairs // devices
    if devices == len(ORDER) + 1 and total % (128 * devices) == 0:
        sources = ORDER + (0,)
        shares = pieces(spectra, block_counts, window_masks, devices, sources[:FIRST], "pack_first")
        shares += pieces(spectra, block_counts, window_masks, devices, sources[FIRST:], "pack_rest")
        blocks = swap(shares, sources, devices)
    else:
        packed = pack(spectra, block_counts, window_masks, devices)
        sources = (None,)
        blocks = [lax.all_to_all(packed, "sta", split_axis=0, concat_axis=0, tiled=True)]
    weights = window_masks.astype(jnp.float32)
    joint = jnp.einsum("dwa,dwb->dab", weights, weights)
    inverse = (1.0 / jnp.maximum(joint, 1.0)).reshape(-1)
    if len(sources) > 1:
        late = sources[-1 - LATE : -1]
        soon = [n for n, away in enumerate(sources) if away not in late]
        *started, table = cross(
            [blocks[n] for n in soon],
            tuple(sources[n] for n in soon),
            inverse,
            pair_table,
            devices,
            late,
            table=table,
        )
        shares = cross(
            blocks[-1 - LATE : -1], late, inverse, pair_table, devices, (), tuple(started)
        )[2:]
        sources = (0,) + ORDER
        received = swap(shares, sources, devices)
    else:
        stacked, _ = cross(blocks, sources, inverse, pair_table, devices)
        received = [lax.all_to_all(stacked, "sta", split_axis=0, concat_axis=0, tiled=True)]
    scale = 1.0 / math.sqrt(total)
    if len(sources) > 1:
        kept = len(sources) - LATE
        started = lags(received[:kept], sources[:kept], table, scale, sources[kept:])
        lagged = lags(received[kept:], sources[kept:], table, scale, (), tuple(started))
    else:
        lagged = lags(received, sources, table, scale)
    return lagged.reshape(rounds, held, slots * slots, LAGS)


def solution(mesh):
    placed = (P(None, "grp", None, "sta", None), P(), P("grp", None, None), P())

    def run(spectra, block_counts, window_masks, pair_table):
        table = phase_tiles(spectra.shape[-1], LAGS, 256)
        return jax.shard_map(
            functools.partial(local, table),
            mesh=mesh,
            in_specs=placed,
            out_specs=P("grp", "sta", None, None),
            check_vma=False,
        )(spectra, block_counts, window_masks, pair_table)

    return run
```

```python
import functools
import math

import jax
import jax.numpy as jnp
import ml_dtypes
import numpy as np
from jax import lax
from jax.experimental import pallas as pl
from jax.experimental.pallas import tpu as pltpu
from jax.sharding import PartitionSpec as P

LAGS = 2048
MIB = 1 << 20
ORDER = (12, 1, 13, 2, 14, 3, 15, 4, 9, 5, 10, 6, 11, 7, 8)
FIRST = 2
BACK = (12, 4, 13, 5, 14, 6, 15, 7, 8, 1, 9, 2, 10, 3, 11)
LATE = 3


def phase_tiles(freq_count, lag_count, tile):
    freqs = np.arange(freq_count, dtype=np.int64)
    shifts = np.arange(lag_count // 2, dtype=np.int64)
    phases = np.mod(freqs[:, None] * shifts[None, :], 2 * freq_count)
    angles = np.arange(2 * freq_count) * (math.pi / freq_count)
    cosines = np.cos(angles).astype(np.float32).astype(ml_dtypes.bfloat16)[phases]
    sines = (-np.sin(angles)).astype(np.float32).astype(ml_dtypes.bfloat16)[phases]
    both = np.stack([cosines, sines]).reshape(2, freq_count, -1, tile)
    return np.ascontiguousarray(both.transpose(2, 0, 1, 3))


def pack_kernel(
    devices, counts_ref, masks_ref, spectra_ref, out_ref, raw_ref, rows_ref, ready_ref, in_sems, out_sems
):
    me = lax.axis_index("sta")
    parts, days, windows, slots, _ = spectra_ref.shape
    bins = out_ref.shape[-1]
    count = counts_ref[me]

    def load(step):
        c, d = step // days, step % days
        return pltpu.make_async_copy(spectra_ref.at[c, d], raw_ref.at[c, d], in_sems.at[step])

    def store(step):
        c, d = step // days, step % days
        return pltpu.make_async_copy(ready_ref.at[:, c, d], out_ref.at[:, c, d], out_sems.at[step])

    for step in range(parts * days):
        load(step).start()
    lane = lax.broadcasted_iota(jnp.int32, masks_ref.shape[1:], 1)

    def one(step, carry):
        c, d = step // days, step % days
        mine = jnp.where(lane == me, masks_ref[d], 0)
        keep = (jnp.sum(mine, axis=1, keepdims=True) > 0).astype(jnp.float32)
        load(step).wait()
        for owner in range(devices):
            for w in range(windows):
                rows_ref[owner, w * slots : (w + 1) * slots, :] = raw_ref[
                    c, d, w, :, owner * bins : (owner + 1) * bins
                ].astype(jnp.float32)
        for slot in range(slots):
            live = keep * jnp.where(slot < count, 1.0, 0.0)
            wide = jnp.broadcast_to(live, (windows, bins))
            for owner in range(devices):
                picked = rows_ref[owner, pl.ds(slot, windows, stride=slots), :]
                ready_ref[owner, c, d, slot] = (picked * wide).astype(jnp.bfloat16)
        store(step).start()
        return carry

    lax.fori_loop(0, parts * days, one, 0)
    for step in range(parts * days):
        store(step).wait()


def piece_kernel(aways, counts_ref, masks_ref, spectra_ref, *refs):
    out_refs, (raw_ref, rows_ref, held_ref, number_ref, sems) = refs[: len(aways)], refs[len(aways) :]
    me = lax.axis_index("sta")
    parts, days, windows, slots, bins = raw_ref.shape[1:]
    small = [
        pltpu.make_async_copy(counts_ref, number_ref, sems.at[len(aways)]),
        pltpu.make_async_copy(masks_ref, held_ref, sems.at[len(aways) + 1]),
    ]
    for copy in small:
        copy.start()
    loads = []
    for n, away in enumerate(aways):
        columns = pl.ds(pl.multiple_of((me ^ away) * bins, 128), bins)
        loads.append(
            pltpu.make_async_copy(spectra_ref.at[:, :, :, :, columns], raw_ref.at[n], sems.at[n])
        )
        loads[n].start()
    for copy in small:
        copy.wait()
    count = number_ref[me]
    lane = lax.broadcasted_iota(jnp.int32, masks_ref.shape[1:], 1)
    wide = []
    for d in range(days):
        mine = jnp.where(lane == me, held_ref[d], 0)
        keep = (jnp.sum(mine, axis=1, keepdims=True) > 0).astype(jnp.float32)
        wide.append(jnp.broadcast_to(keep, (windows, bins)))
    live = [jnp.where(slot < count, 1.0, 0.0) for slot in range(slots)]
    for n, out_ref in enumerate(out_refs):
        loads[n].wait()

        def one(c, carry):
            for d in range(days):
                for w in range(windows):
                    rows_ref[d, w * slots : (w + 1) * slots, :] = raw_ref[n, c, d, w].astype(
                        jnp.float32
                    )
                for slot in range(slots):
                    picked = rows_ref[d, pl.ds(slot, windows, stride=slots), :]
                    out_ref[c, d, slot] = (picked * (wide[d] * live[slot])).astype(jnp.bfloat16)
            return carry

        lax.fori_loop(0, parts, one, 0)


def pieces(spectra, block_counts, window_masks, devices, aways, name):
    parts, days, windows, slots, total = spectra.shape
    bins = total // devices
    share = jax.ShapeDtypeStruct((parts, days, slots, windows, bins), jnp.bfloat16)
    return pl.pallas_call(
        functools.partial(piece_kernel, aways),
        in_specs=[
            pl.BlockSpec(memory_space=pl.ANY),
            pl.BlockSpec(memory_space=pl.ANY),
            pl.BlockSpec(memory_space=pl.ANY),
        ],
        out_specs=[pl.BlockSpec(memory_space=pltpu.VMEM)] * len(aways),
        out_shape=[share] * len(aways),
        scratch_shapes=[
            pltpu.VMEM((len(aways), parts, days, windows, slots, bins), jnp.bfloat16),
            pltpu.VMEM((days, windows * slots, bins), jnp.float32),
            pltpu.VMEM(window_masks.shape, jnp.int32),
            pltpu.SMEM(block_counts.shape, jnp.int32),
            pltpu.SemaphoreType.DMA((len(aways) + 2,)),
        ],
        compiler_params=pltpu.CompilerParams(vmem_limit_bytes=60 * MIB),
        name=name,
    )(block_counts, window_masks, spectra)


def pack(spectra, block_counts, window_masks, devices):
    parts, days, windows, slots, total = spectra.shape
    bins = total // devices
    packed = (devices, parts, days, slots, windows, bins)
    return pl.pallas_call(
        functools.partial(pack_kernel, devices),
        in_specs=[
            pl.BlockSpec(memory_space=pltpu.SMEM),
            pl.BlockSpec(memory_space=pltpu.VMEM),
            pl.BlockSpec(memory_space=pl.ANY),
        ],
        out_specs=pl.BlockSpec(memory_space=pl.ANY),
        out_shape=jax.ShapeDtypeStruct(packed, jnp.bfloat16),
        scratch_shapes=[
            pltpu.VMEM(spectra.shape, jnp.bfloat16),
            pltpu.VMEM((devices, windows * slots, bins), jnp.float32),
            pltpu.VMEM(packed, jnp.bfloat16),
            pltpu.SemaphoreType.DMA((parts * days,)),
            pltpu.SemaphoreType.DMA((parts * days,)),
        ],
        compiler_params=pltpu.CompilerParams(vmem_limit_bytes=60 * MIB),
        name="pack",
    )(block_counts, window_masks, spectra)


def window_sums(terms, rows):
    for step in (1, 2, 4):
        own = (rows & step) == 0
        terms = [
            jnp.where(own, first, second) + pltpu.roll(jnp.where(own, second, first), 8 - step, 0)
            for first, second in zip(terms[::2], terms[1::2])
        ]
    return terms[0]


def pair_stack(a, b, inverse_ref, blocks_ref, rows):
    block_count, _, days, slots = blocks_ref.shape[:4]
    total = None
    stacked = []
    for d in range(days):
        scale = inverse_ref[(d * block_count + a) * block_count + b]
        right = [[blocks_ref[b, c, d, s].astype(jnp.float32) for s in range(slots)] for c in range(2)]
        right_sum = [x + y for x, y in zip(right[0], right[1])]
        right_gap = [y - x for x, y in zip(right[0], right[1])]
        real, imag = [], []
        for i in range(slots):
            left_real = blocks_ref[a, 0, d, i].astype(jnp.float32)
            left_imag = blocks_ref[a, 1, d, i].astype(jnp.float32)
            left_sum = left_real + left_imag
            for j in range(slots):
                shared = left_sum * right[0][j]
                gain = left_imag * right_gap[j]
                loss = left_real * right_sum[j]
                both = shared[:8] + shared[8:]
                real.append(both + (gain[:8] + gain[8:]))
                imag.append(both - (loss[:8] + loss[8:]))
        fresh = [
            [window_sums(part[k : k + 8], rows) * scale for k in range(0, slots * slots, 8)]
            for part in (real, imag)
        ]
        if total is None:
            total = fresh
        else:
            total = [[t + n for t, n in zip(ts, ns)] for ts, ns in zip(total, fresh)]
        stacked.append([jnp.concatenate(part, axis=0).astype(jnp.bfloat16) for part in total])
    return stacked


def cross_kernel(sources, late, aliased, rounds, pairs, pairs_ref, inverse_ref, *refs):
    block_refs, refs = refs[: len(sources)], refs[len(sources) + aliased :]
    if late:
        table_ref, out_ref, blocks_ref, held_ref, sem = refs
        share_refs = ()
        fetch = pltpu.make_async_copy(table_ref, held_ref, sem)
        fetch.start()
    else:
        out_ref, blocks_ref, *share_refs = refs
    block_count, _, days, slots, _, bins = blocks_ref.shape
    rows = lax.broadcasted_iota(jnp.int32, (8, bins), 0)
    held = days * pairs // block_count
    me = lax.axis_index("sta")
    for ref, source in zip(block_refs, sources):
        if source is None:

            def widen(n, carry):
                blocks_ref[n] = ref[n].astype(jnp.float32)
                return carry

            lax.fori_loop(0, block_count, widen, 0)
        else:
            blocks_ref[me ^ source] = ref[...].astype(jnp.float32)

    def one_pair(r, p):
        a = pairs_ref[(r * pairs + p) * 2]
        b = pairs_ref[(r * pairs + p) * 2 + 1]

        def work():
            stacked = pair_stack(a, b, inverse_ref, blocks_ref, rows)
            for d in range(days):
                row = pl.multiple_of((r * held + d % held) * slots * slots, 16)
                for c in range(2):
                    out_ref[(p * days + d) // held, c, pl.ds(row, slots * slots), :] = stacked[d][c]

        if late:
            waits = [(x ^ me) == away for x in (a, b) for away in late]
            pl.when(jnp.logical_not(functools.reduce(jnp.logical_or, waits)))(work)
        else:
            work()

    def any_pair(index, carry):
        one_pair(index // pairs, index % pairs)
        return carry

    def late_pairs(r, carry):
        for source in sources:
            one_pair(r, pairs_ref[(rounds * pairs) * 2 + r * block_count + (me ^ source)])
        return carry

    if aliased:
        lax.fori_loop(0, rounds, late_pairs, 0)
    else:
        lax.fori_loop(0, rounds * pairs, any_pair, 0)
    for share_ref, away in zip(share_refs, (0,) + BACK):
        share_ref[...] = out_ref[me ^ away]
    if late:
        fetch.wait()


def cross(blocks, sources, inverse, pair_table, devices, late=(), started=(), table=None):
    parts, days, slots, windows, bins = blocks[0].shape[-5:]
    rounds, pairs, _ = pair_table.shape
    held = days * pairs // devices
    share = len(sources) / devices
    stack = rounds * held * slots * slots
    spread = devices if started else 0
    tables = [] if table is None else [table]
    blocks_of = pair_table[..., None] == jnp.arange(devices, dtype=jnp.int32)
    owner = jnp.sum(blocks_of * jnp.arange(pairs, dtype=jnp.int32)[:, None, None], axis=(1, 2))
    wide = 4 * devices * parts * days * slots * windows * max(bins, 128)
    work = int(rounds * pairs * days * slots * slots * windows * bins * share)
    return pl.pallas_call(
        functools.partial(cross_kernel, sources, late, len(started), rounds, pairs),
        in_specs=[pl.BlockSpec(memory_space=pltpu.SMEM)] * 2
        + [pl.BlockSpec(memory_space=pltpu.VMEM)] * (len(blocks) + len(started))
        + [pl.BlockSpec(memory_space=pl.ANY)] * len(tables),
        out_specs=[pl.BlockSpec(memory_space=pltpu.VMEM)] * (2 + spread + len(tables)),
        out_shape=[
            jax.ShapeDtypeStruct((devices, parts, stack, bins), jnp.bfloat16),
            jax.ShapeDtypeStruct((devices, parts, days, slots, windows, bins), jnp.float32),
        ]
        + [jax.ShapeDtypeStruct((parts, stack, bins), jnp.bfloat16)] * spread
        + [jax.ShapeDtypeStruct(table.shape, table.dtype) for table in tables],
        scratch_shapes=[pltpu.SemaphoreType.DMA] * len(tables),
        input_output_aliases={2 + len(blocks) + n: n for n in range(len(started))},
        compiler_params=pltpu.CompilerParams(vmem_limit_bytes=38 * MIB if late else wide + 20 * MIB),
        cost_estimate=pl.CostEstimate(
            flops=16 * work, bytes_accessed=4 << 20, transcendentals=0
        ),
        name="cross_rest" if started else "cross",
    )(jnp.concatenate([pair_table.reshape(-1), owner.reshape(-1)]), inverse, *blocks, *started, *tables)


def quarter_turns(depth):
    turn = lax.broadcasted_iota(jnp.int32, (depth, 128), 0) % 4
    cosine = jnp.where(turn == 0, 1.0, jnp.where(turn == 2, -1.0, 0.0))
    sine = jnp.where(turn == 1, 1.0, jnp.where(turn == 3, -1.0, 0.0))
    return cosine.astype(jnp.bfloat16), sine.astype(jnp.bfloat16)


def product(left, right):
    return jnp.dot(left, right, preferred_element_type=jnp.float32)


def write_lags(scale, sums, before, out_ref, lagged_ref, out_sems):
    rows, lag_count = lagged_ref.shape
    tiles = out_sems.shape[0] // 2
    half = lag_count // 2
    tile = half // tiles
    lane = lax.broadcasted_iota(jnp.int32, (rows, 128), 1)
    flip = (128 - lane) % 128
    before = before * scale
    stores = []
    for t in reversed(range(tiles)):
        even, odd = sums(t)
        even, odd = even * scale, odd * scale
        lagged_ref[:, half + t * tile : half + (t + 1) * tile] = even + odd
        gap = even - odd
        for sub in reversed(range(tile // 128)):
            turned = jnp.take_along_axis(gap[:, sub * 128 : (sub + 1) * 128], flip, axis=1)
            at = half - t * tile - (sub + 1) * 128
            lagged_ref[:, at : at + 128] = jnp.where(lane == 0, before, turned)
            before = turned
        for k, at in enumerate((half + t * tile, half - (t + 1) * tile)):
            stores.append(
                pltpu.make_async_copy(
                    lagged_ref.at[:, at : at + tile],
                    out_ref.at[:, at : at + tile],
                    out_sems.at[2 * t + k],
                )
            )
            stores[-1].start()
    for store in stores:
        store.wait()


def place(source, bins):
    return pl.ds(pl.multiple_of((lax.axis_index("sta") ^ source) * bins, 128), bins)


def lag_kernel(scale, sources, late, *refs):
    stacked_refs, table_ref, refs = refs[: len(sources)], refs[len(sources)], refs[len(sources) + 1 :]
    tiles, parts, depth, tile = table_ref.shape
    left_ref = refs[2]
    rows = left_ref.shape[1]
    for stacked_ref, source in zip(stacked_refs, sources):
        bins = stacked_ref.shape[-1]
        for c in range(parts):
            if source is None:
                for src in range(stacked_ref.shape[0]):
                    left_ref[c, :, src * bins : (src + 1) * bins] = stacked_ref[src, c]
            else:
                left_ref[c, :, place(source, bins)] = stacked_ref[c]
    for source in late:
        for c in range(parts):
            left_ref[c, :, place(source, bins)] = jnp.zeros((rows, bins), jnp.bfloat16)

    cosine, sine = quarter_turns(depth)
    before = product(left_ref[0], cosine) + product(left_ref[1], sine)

    def sums(t):
        return product(left_ref[0], table_ref[t, 0]), product(left_ref[1], table_ref[t, 1])

    if late:
        sums_ref, before_ref, _ = refs
        before_ref[...] = before
        for t in range(tiles):
            sums_ref[t, 0], sums_ref[t, 1] = sums(t)
    else:
        out_ref, lagged_ref, _, out_sems = refs
        write_lags(scale, sums, before, out_ref, lagged_ref, out_sems)


def rest_kernel(scale, sources, *refs):
    stacked_refs, refs = refs[: len(sources)], refs[len(sources) :]
    table_ref, sums_ref, before_ref, out_ref, lagged_ref, out_sems = refs
    bins = stacked_refs[0].shape[-1]
    cosine, sine = quarter_turns(bins)
    before = before_ref[...]
    for ref in stacked_refs:
        before = before + (product(ref[0], cosine) + product(ref[1], sine))

    def sums(t):
        totals = []
        for c in range(2):
            total = sums_ref[t, c]
            for ref, source in zip(stacked_refs, sources):
                total = total + product(ref[c], table_ref[t, c, place(source, bins), :])
            totals.append(total)
        return totals

    write_lags(scale, sums, before, out_ref, lagged_ref, out_sems)


def lags(stacked, sources, table, scale, late=(), started=()):
    parts, rows, _ = stacked[0].shape[-3:]
    tiles, _, depth, tile = table.shape
    lag_count = 2 * tiles * tile
    vmem = pl.BlockSpec(memory_space=pltpu.VMEM)
    left = pltpu.VMEM((parts, rows, depth), jnp.bfloat16)
    if late:
        body = functools.partial(lag_kernel, scale, sources, late)
        out_specs = [vmem] * 2
        out_shape = [
            jax.ShapeDtypeStruct((tiles, parts, rows, tile), jnp.float32),
            jax.ShapeDtypeStruct((rows, 128), jnp.float32),
        ]
        scratch = [left]
    else:
        out_specs = pl.BlockSpec(memory_space=pl.ANY)
        out_shape = jax.ShapeDtypeStruct((rows, lag_count), jnp.float32)
        scratch = [pltpu.VMEM((rows, lag_count), jnp.float32)]
        if started:
            body = functools.partial(rest_kernel, scale, sources)
        else:
            body = functools.partial(lag_kernel, scale, sources, late)
            scratch.append(left)
        scratch.append(pltpu.SemaphoreType.DMA((2 * tiles,)))
    return pl.pallas_call(
        body,
        in_specs=[vmem] * (len(stacked) + 1 + len(started)),
        out_specs=out_specs,
        out_shape=out_shape,
        scratch_shapes=scratch,
        compiler_params=pltpu.CompilerParams(vmem_limit_bytes=20 * MIB),
        cost_estimate=pl.CostEstimate(
            flops=2 * rows * depth * lag_count, bytes_accessed=4 << 20, transcendentals=0
        ),
        name="lags_first" if late else "lags",
    )(*stacked, table, *started)


def swap(shares, sources, devices):
    received = []
    sent = []
    for share, away in zip(shares, sources):
        if away:
            if len(sent) >= 5:
                share, _ = lax.optimization_barrier((share, sent[-5]))
            share = lax.ppermute(share, "sta", [(n, n ^ away) for n in range(devices)])
            sent.append(share)
        received.append(share)
    return received


def local(table, spectra, block_counts, window_masks, pair_table):
    devices = lax.axis_size("sta")
    parts, days, windows, slots, total = spectra.shape
    rounds, pairs, _ = pair_table.shape
    held = days * pairs // devices
    if devices == len(ORDER) + 1 and total % (128 * devices) == 0:
        sources = ORDER + (0,)
        shares = pieces(spectra, block_counts, window_masks, devices, sources[:FIRST], "pack_first")
        shares += pieces(spectra, block_counts, window_masks, devices, sources[FIRST:], "pack_rest")
        blocks = swap(shares, sources, devices)
    else:
        packed = pack(spectra, block_counts, window_masks, devices)
        sources = (None,)
        blocks = [lax.all_to_all(packed, "sta", split_axis=0, concat_axis=0, tiled=True)]
    weights = window_masks.astype(jnp.float32)
    joint = jnp.einsum("dwa,dwb->dab", weights, weights)
    inverse = (1.0 / jnp.maximum(joint, 1.0)).reshape(-1)
    if len(sources) > 1:
        late = sources[-1 - LATE : -1]
        soon = [n for n, away in enumerate(sources) if away not in late]
        *started, table = cross(
            [blocks[n] for n in soon],
            tuple(sources[n] for n in soon),
            inverse,
            pair_table,
            devices,
            late,
            table=table,
        )
        shares = cross(
            blocks[-1 - LATE : -1], late, inverse, pair_table, devices, (), tuple(started)
        )[2:]
        sources = (0,) + BACK
        received = swap(shares, sources, devices)
    else:
        stacked, _ = cross(blocks, sources, inverse, pair_table, devices)
        received = [lax.all_to_all(stacked, "sta", split_axis=0, concat_axis=0, tiled=True)]
    scale = 1.0 / math.sqrt(total)
    if len(sources) > 1:
        kept = len(sources) - LATE
        started = lags(received[:kept], sources[:kept], table, scale, sources[kept:])
        lagged = lags(received[kept:], sources[kept:], table, scale, (), tuple(started))
    else:
        lagged = lags(received, sources, table, scale)
    return lagged.reshape(rounds, held, slots * slots, LAGS)


def solution(mesh):
    placed = (P(None, "grp", None, "sta", None), P(), P("grp", None, None), P())

    def run(spectra, block_counts, window_masks, pair_table):
        table = phase_tiles(spectra.shape[-1], LAGS, 256)
        return jax.shard_map(
            functools.partial(local, table),
            mesh=mesh,
            in_specs=placed,
            out_specs=P("grp", "sta", None, None),
            check_vma=False,
        )(spectra, block_counts, window_masks, pair_table)

    return run
```
